128 devices in a mesh: seq: 64 (over x, z, y), head: 2 (over core).
Axes of the slice: x: 4, y: 4, z: 4, core: 2. Of those that a mesh axis runs over, the one named last changes fastest.
Arguments:
- prompt_x: bfloat16 [64, 512, 8192], P('seq', None, 'head'), may hold values from -6 to 6
- prompt_b: bfloat16 [64, 512, 512], P('seq', None, 'head'), may hold values from -6 to 6
- prompt_dt: bfloat16 [64, 128, 512], P('seq', 'head'), may hold values from -4 to 4
- prompt_keys: bfloat16 [64, 512, 512], P('seq', None, 'head'), may hold values from -6 to 6
- prompt_values: bfloat16 [64, 512, 512], P('seq', None, 'head'), may hold values from -6 to 6
- prompt_len: int32 [64], P('seq'), may hold values from 1 to 512, 24576 in all
- reply_x: bfloat16 [128, 128, 8192], P('seq', None, 'head'), may hold values from -6 to 6
- reply_b: bfloat16 [128, 128, 512], P('seq', None, 'head'), may hold values from -6 to 6
- reply_c: bfloat16 [128, 128, 512], P('seq', None, 'head'), may hold values from -0.5 to 0.5
- reply_dt: bfloat16 [128, 128, 128], P('seq', 'head'), may hold values from -4 to 4
- reply_queries: bfloat16 [128, 128, 4096], P('seq', None, 'head'), may hold values from -6 to 6
- reply_keys: bfloat16 [128, 128, 512], P('seq', None, 'head'), may hold values from -6 to 6
- reply_values: bfloat16 [128, 128, 512], P('seq', None, 'head'), may hold values from -6 to 6
- reply_len: int32 [128], P('seq'), may hold values from 1 to 128, 10240 in all
- reply_owner: int32 [128], P('seq'), may hold values from 0 to 63, as said below
- decay_log: float32 [128], P('head'), may hold values from -4.5 to 0.5
- step_bias: float32 [128], P('head'), may hold values from -5 to -2.5
- norm_gain: float32 [8192], P('head'), may hold values from 0.5 to 1.5
- ssm_cotangent: bfloat16 [128, 128, 8192], P('seq', None, 'head'), may hold values from -6 to 6
- attn_cotangent: bfloat16 [128, 128, 4096], P('seq', None, 'head'), may hold values from -6 to 6
Outputs:
- ssm_output: bfloat16 [128, 128, 8192], P('seq', None, 'head')
- attn_output: bfloat16 [128, 128, 4096], P('seq', None, 'head')
- grad_reply_x: bfloat16 [128, 128, 8192], P('seq', None, 'head')
- grad_reply_b: bfloat16 [128, 128, 512], P('seq', None, 'head')
- grad_reply_c: bfloat16 [128, 128, 512], P('seq', None, 'head')
- grad_reply_dt: bfloat16 [128, 128, 128], P('seq', 'head')
- grad_queries: bfloat16 [128, 128, 4096], P('seq', None, 'head')
- grad_reply_keys: bfloat16 [128, 128, 512], P('seq', None, 'head')
- grad_reply_values: bfloat16 [128, 128, 512], P('seq', None, 'head')
- grad_prompt_x: bfloat16 [64, 512, 8192], P('seq', None, 'head')
- grad_prompt_b: bfloat16 [64, 512, 512], P('seq', None, 'head')
- grad_prompt_dt: bfloat16 [64, 128, 512], P('seq', 'head')
- grad_prompt_keys: bfloat16 [64, 512, 512], P('seq', None, 'head')
- grad_prompt_values: bfloat16 [64, 512, 512], P('seq', None, 'head')
The draws below stay inside these ranges and needn't reach their ends.
Inputs may be any that keep to these rules, and one draw needn't show every extreme that they name: Response r sits on index r // 2 of seq; its prompt reply_owner[r] lies k indices before it along seq, counted cyclically modulo 64, for some k from 1 to 3.
All inputs are finite; a program needn't handle non-finite values. No bound on the sum of `prompt_len` or of `reply_len` on one device may be relied on, other than what follows from the above.
Results may differ from the reference program's by a relative error of at most 0.0028.
Values sent between devices are 32-bit elements; how exact they have to be, the bound alone decides.
No kernel may reach another device: no remote copies, remote signals or barrier semaphores. Data moves between devices by JAX's collectives and lax.ppermute only.
A program may use at most 192 MiB of HBM per device.

```python
import math
import jax
import jax.numpy as jnp
import numpy as np
from jax import lax

HEADS = 128
HDIM = 64
STATE = 128
GROUPS = 4
QHEADS = 32
KVHEADS = 4
AHDIM = 128
OFFSETS = 3
LP = 512
LR = 128
RESP_DEV = 2
PROMPTS = 64
RESPONSES = 128


def draw_reply_queries(key, part):
    key = jax.random.fold_in(key, 3)
    array_shape = (RESPONSES, LR, QHEADS * AHDIM)
    drawn = jnp.clip(jax.random.normal(key, array_shape, jnp.float32), -6.0, 6.0)
    return drawn.astype(jnp.bfloat16)


def draw_reply_keys(key, part):
    key = jax.random.fold_in(key, 5)
    array_shape = (RESPONSES, LR, KVHEADS * AHDIM)
    drawn = jnp.clip(jax.random.normal(key, array_shape, jnp.float32), -6.0, 6.0)
    return drawn.astype(jnp.bfloat16)


def draw_prompt_keys(key, part):
    key = jax.random.fold_in(key, 9)
    array_shape = (PROMPTS, LP, KVHEADS * AHDIM)
    drawn = jnp.clip(jax.random.normal(key, array_shape, jnp.float32), -6.0, 6.0)
    return drawn.astype(jnp.bfloat16)


def draw_reply_owner(key, part):
    key = jax.random.fold_in(key, 7)
    position = jnp.arange(RESPONSES, dtype=jnp.int32)
    device = position // RESP_DEV
    offset = 1 + jax.random.randint(key, (RESPONSES,), 0, OFFSETS, dtype=jnp.int32)
    leading = (position % RESP_DEV == 0) & (device >= 1) & (device <= OFFSETS)
    offset = jnp.where(leading, device, offset)
    offset = jnp.where(position == 0, 1, offset)
    return ((device - offset) % PROMPTS).astype(jnp.int32)


def block_scale(rng, dims, split, low, top_value):
    def one(dim, parts):
        draws = jax.random.uniform(jax.random.fold_in(jax.random.fold_in(rng, 6), dim), (parts,), jnp.float32, low / len(split), top_value / len(split))
        return jnp.repeat(jnp.exp(draws), dims[dim] // parts).reshape((-1,) + (1,) * (len(dims) - dim - 1))

    loudness = one(*split[0])
    for cut in split[1:]:
        loudness = loudness * one(*cut)
    return loudness


def split_up(number_of, total, reach, lean):
    loads = [(1 << 20) // math.isqrt(grade ** lean) + 1 for grade in range(2, number_of + 1)]
    surplus, given = total - reach - (number_of - 1), [1] * (number_of - 1)
    while surplus > 0:
        candidates = [i for i in range(number_of - 1) if given[i] < reach]
        mass, budget = sum([loads[i] for i in candidates]), surplus
        for i in candidates:
            addition = min(reach - given[i], max(1, budget * loads[i] // mass), surplus)
            given[i] = given[i] + addition
            surplus = surplus - addition
    return np.array([reach] + given)


def uneven_parts(rng, number_of, total, reach, slope):
    if number_of == 2:
        one = jax.random.randint(rng, (), max(1, total - reach), min(reach, total - 1) + 1)
        return jnp.stack([one, total - one])
    tallies = jnp.asarray(split_up(number_of, total, reach, slope), jnp.int32)
    twos = (number_of - 1) // 2
    donor, taker = tallies[1:1 + 2 * twos:2], tallies[2:2 + 2 * twos:2]
    room = jnp.minimum(donor - 1, reach - taker)
    shifted = jax.random.randint(jax.random.fold_in(rng, 1), (twos,), 0, 1 << 20) % (room + 1)
    tallies = tallies.at[1:1 + 2 * twos:2].set(donor - shifted).at[2:2 + 2 * twos:2].set(taker + shifted)
    return tallies[jax.random.permutation(jax.random.fold_in(rng, 2), number_of)]


def bell_draw(stream_key, shape, width, most, split=(), kind=jnp.bfloat16):
    values = width * jax.random.normal(stream_key, shape, jnp.float32)
    if split:
        values = values * block_scale(stream_key, shape, split, -0.22, 0.18)
    return jnp.clip(values, -most, most).astype(kind)


def setup_inputs(seed: int = 0) -> dict:
    key_list = jax.random.split(jax.random.key(seed), 21)
    prompt_x = bell_draw(key_list[0], (PROMPTS, LP, HEADS * HDIM), 1.0, 6.0, ((0, 64), (2, 2)))
    prompt_b = bell_draw(key_list[1], (PROMPTS, LP, GROUPS * STATE), 1.0, 6.0, ((0, 64), (2, 2)))
    prompt_dt = bell_draw(key_list[2], (PROMPTS, HEADS, LP), 1.0, 4.0, ((0, 64), (1, 2)))
    prompt_keys = draw_prompt_keys(jax.random.fold_in(key_list[20], 71), 0)
    prompt_values = bell_draw(key_list[4], (PROMPTS, LP, KVHEADS * AHDIM), 1.0, 6.0, ((0, 64), (2, 2)))
    prompt_len = uneven_parts(key_list[5], PROMPTS, PROMPTS * LP * 3 // 4, LP, 1).astype(jnp.int32)
    reply_x = bell_draw(key_list[6], (RESPONSES, LR, HEADS * HDIM), 1.0, 6.0, ((0, 64), (2, 2)))
    reply_b = bell_draw(key_list[7], (RESPONSES, LR, GROUPS * STATE), 1.0, 6.0, ((0, 64), (2, 2)))
    reply_c = bell_draw(key_list[8], (RESPONSES, LR, GROUPS * STATE), STATE ** -0.5, 0.5, ((0, 64), (2, 2)))
    reply_dt = bell_draw(key_list[9], (RESPONSES, HEADS, LR), 1.0, 4.0, ((0, 64), (1, 2)))
    reply_queries = draw_reply_queries(jax.random.fold_in(key_list[20], 71), 0)
    reply_keys = draw_reply_keys(jax.random.fold_in(key_list[20], 71), 0)
    reply_values = bell_draw(key_list[12], (RESPONSES, LR, KVHEADS * AHDIM), 1.0, 6.0, ((0, 64), (2, 2)))
    reply_len = uneven_parts(key_list[13], RESPONSES, RESPONSES * LR * 5 // 8, LR, 2).astype(jnp.int32)
    reply_owner = draw_reply_owner(jax.random.fold_in(key_list[20], 71), 0)
    decay_log = jnp.clip(-4.5 + 5.0 * jax.random.uniform(key_list[15], (HEADS,), jnp.float32) ** block_scale(key_list[15], (HEADS,), ((0, 2),), -0.2, 0.2), -4.5, 0.5)
    step_bias = jnp.clip(-5.0 + 2.5 * jax.random.uniform(key_list[16], (HEADS,), jnp.float32) ** block_scale(key_list[16], (HEADS,), ((0, 2),), -0.2, 0.2), -5.0, -2.5)
    norm_gain = jnp.clip(1.0 + 0.1 * jax.random.normal(key_list[17], (HEADS * HDIM,), jnp.float32), 0.5, 1.5)
    ssm_cotangent = bell_draw(key_list[18], (RESPONSES, LR, HEADS * HDIM), 1.0, 6.0, ((0, 64), (2, 2)))
    attn_cotangent = bell_draw(key_list[19], (RESPONSES, LR, QHEADS * AHDIM), 1.0, 6.0, ((0, 64), (2, 2)))
    return {"prompt_x": prompt_x, "prompt_b": prompt_b, "prompt_dt": prompt_dt, "prompt_keys": prompt_keys, "prompt_values": prompt_values, "prompt_len": prompt_len, "reply_x": reply_x, "reply_b": reply_b, "reply_c": reply_c, "reply_dt": reply_dt, "reply_queries": reply_queries, "reply_keys": reply_keys, "reply_values": reply_values, "reply_len": reply_len, "reply_owner": reply_owner, "decay_log": decay_log, "step_bias": step_bias, "norm_gain": norm_gain, "ssm_cotangent": ssm_cotangent, "attn_cotangent": attn_cotangent}


HIGHEST = lax.Precision.HIGHEST

def prefix_state(x_part, b_part, dt_part, prior_length, decay_log, step_bias):
    head_count = dt_part.shape[0]
    length = dt_part.shape[1]
    groups = b_part.shape[1] // STATE
    per_group = head_count // groups
    validity = (jnp.arange(length) < prior_length).astype(jnp.float32)
    step_sizes = jax.nn.softplus(dt_part.astype(jnp.float32) + step_bias[:, None]) * validity[None, :]
    decay_rate = -jnp.exp(decay_log)
    running = jnp.cumsum(step_sizes, axis=1)
    weight = step_sizes * jnp.exp(decay_rate[:, None] * (running[:, -1:] - running))
    x_wide = x_part.astype(jnp.float32).reshape(length, groups, per_group, HDIM)
    b_wide = b_part.astype(jnp.float32).reshape(length, groups, STATE)
    result = jnp.einsum('gjs,sgjp,sgn->gjpn', weight.reshape(groups, per_group, length), x_wide, b_wide, precision=HIGHEST)
    return result.reshape(head_count, HDIM, STATE)

def reply_forward(x_part, b_part, c_part, dt_part, q_part, k_part, v_part, reply_length, carried_state, prior_keys, prior_values, prior_length, decay_log, step_bias):
    head_count, length = dt_part.shape
    groups = b_part.shape[1] // STATE
    per_group = head_count // groups
    validity = (jnp.arange(length) < reply_length).astype(jnp.float32)
    step_sizes = jax.nn.softplus(dt_part.astype(jnp.float32) + step_bias[:, None]) * validity[None, :]
    decay_rate = -jnp.exp(decay_log)
    running = jnp.cumsum(step_sizes, axis=1)
    causal = jnp.arange(length)[:, None] >= jnp.arange(length)[None, :]
    exponent = decay_rate[:, None, None] * (running[:, :, None] - running[:, None, :])
    decay_table = jnp.where(causal[None], jnp.exp(jnp.where(causal[None], exponent, 0.0)), 0.0)
    b_wide = b_part.astype(jnp.float32).reshape(length, groups, STATE)
    c_wide = c_part.astype(jnp.float32).reshape(length, groups, STATE)
    intersection = jnp.einsum('tgn,sgn->gts', c_wide, b_wide, precision=HIGHEST)
    mixing = decay_table.reshape(groups, per_group, length, length) * intersection[:, None] * step_sizes.reshape(groups, per_group, 1, length)
    x_wide = x_part.astype(jnp.float32).reshape(length, groups, per_group, HDIM)
    local_part = jnp.einsum('gjts,sgjp->tgjp', mixing, x_wide, precision=HIGHEST)
    carried = jnp.einsum('tgn,gjpn->tgjp', c_wide, carried_state.reshape(groups, per_group, HDIM, STATE), precision=HIGHEST)
    fading = jnp.exp(decay_rate[:, None] * running).T.reshape(length, groups, per_group, 1)
    ssm_raw = (local_part + carried * fading).reshape(length, head_count * HDIM) * validity[:, None]
    kv_count = k_part.shape[1] // AHDIM
    q_count = q_part.shape[1] // AHDIM
    queries = q_part.astype(jnp.float32).reshape(length, kv_count, q_count // kv_count, AHDIM)
    prior_rows = prior_keys.shape[0]
    all_keys = jnp.concatenate([prior_keys, k_part.astype(jnp.float32)], axis=0).reshape(prior_rows + length, kv_count, AHDIM)
    all_values = jnp.concatenate([prior_values, v_part.astype(jnp.float32)], axis=0).reshape(prior_rows + length, kv_count, AHDIM)
    key_index = jnp.arange(prior_rows + length)[None, :]
    query_index = jnp.arange(length)[:, None]
    own_index = key_index - prior_rows
    allowed = jnp.where(key_index < prior_rows, key_index < prior_length, (own_index <= query_index) & (own_index < reply_length))
    scores = jnp.einsum('tkhd,skd->khts', queries, all_keys, precision=HIGHEST) * AHDIM ** (-0.5)
    scores = jnp.where(allowed[None, None], scores, -1e+30)
    weights = jax.nn.softmax(scores, axis=-1)
    attention = jnp.einsum('khts,skd->tkhd', weights, all_values, precision=HIGHEST).reshape(length, q_count * AHDIM) * validity[:, None]
    return (ssm_raw, attention)

def normalize(ssm_raw, norm_gain):
    mean_square = lax.optimization_barrier(jnp.mean(ssm_raw * ssm_raw, axis=-1, keepdims=True))
    return ssm_raw * lax.rsqrt(mean_square + 1e-05) * norm_gain

def reference(prompt_x, prompt_b, prompt_dt, prompt_keys, prompt_values, prompt_len, reply_x, reply_b, reply_c, reply_dt, reply_queries, reply_keys, reply_values, reply_len, reply_owner, decay_log, step_bias, norm_gain, ssm_cotangent, attn_cotangent):

    def state_of(position):
        return prefix_state(prompt_x[position], prompt_b[position], prompt_dt[position], prompt_len[position], decay_log, step_bias)
    states = lax.map(state_of, jnp.arange(PROMPTS, dtype=jnp.int32))
    keys_wide = prompt_keys.astype(jnp.float32)
    values_wide = prompt_values.astype(jnp.float32)

    def one_reply(position):
        owner_index = reply_owner[position]

        def forward(x_part, b_part, c_part, dt_part, q_part, k_part, v_part, carried_state, prior_keys, prior_values):
            ssm_raw, attention = reply_forward(x_part, b_part, c_part, dt_part, q_part, k_part, v_part, reply_len[position], carried_state, prior_keys, prior_values, prompt_len[owner_index], decay_log, step_bias)
            return (normalize(ssm_raw, norm_gain), attention)
        results, pull_back = jax.vjp(forward, reply_x[position], reply_b[position], reply_c[position], reply_dt[position], reply_queries[position], reply_keys[position], reply_values[position], states[owner_index], keys_wide[owner_index], values_wide[owner_index])
        gradients = pull_back((ssm_cotangent[position].astype(jnp.float32), attn_cotangent[position].astype(jnp.float32)))
        return (results[0].astype(jnp.bfloat16), results[1].astype(jnp.bfloat16)) + tuple(gradients)
    replies = lax.map(one_reply, jnp.arange(RESPONSES, dtype=jnp.int32))
    state_grad = jax.ops.segment_sum(replies[9], reply_owner, num_segments=PROMPTS)
    key_grad = jax.ops.segment_sum(replies[10], reply_owner, num_segments=PROMPTS)
    value_grad = jax.ops.segment_sum(replies[11], reply_owner, num_segments=PROMPTS)

    def prompt_grad(position):

        def forward(x_part, b_part, dt_part):
            return prefix_state(x_part, b_part, dt_part, prompt_len[position], decay_log, step_bias)
        unused, pull_back = jax.vjp(forward, prompt_x[position], prompt_b[position], prompt_dt[position])
        return pull_back(state_grad[position])
    prompt_grads = lax.map(prompt_grad, jnp.arange(PROMPTS, dtype=jnp.int32))
    return (replies[0], replies[1], replies[2], replies[3], replies[4], replies[5], replies[6], replies[7], replies[8], prompt_grads[0], prompt_grads[1], prompt_grads[2], key_grad.astype(jnp.bfloat16), value_grad.astype(jnp.bfloat16))
```

```python
import jax
import jax.numpy as jnp
from jax import lax
from jax.experimental import pallas as pl
from jax.experimental.pallas import tpu as pltpu
from jax.sharding import PartitionSpec as P

HEADS = 128
HDIM = 64
STATE = 128
AHDIM = 128
OFFSETS = 3
LP = 512
LR = 128
MARK = 8
ROW = 4

HIGHEST = lax.Precision.HIGHEST
F32 = jnp.float32
BF16 = jnp.bfloat16


def split(a):
    hi = a.astype(BF16)
    return hi, (a - hi.astype(F32)).astype(BF16)


def dot(a, b, ca, cb):
    return lax.dot_general(a, b, (((ca,), (cb,)), ((), ())), preferred_element_type=F32)


def dot2(a, b, ca, cb):
    hi, lo = split(a)
    return dot(hi, b, ca, cb) + dot(lo, b, ca, cb)


def dot3(a, b, ca, cb):
    return dot(a[0], b[0], ca, cb) + (dot(a[1], b[0], ca, cb) + dot(a[0], b[1], ca, cb))


def spread(columns, lower):
    parts = []
    for pair in range(columns.shape[1] // 2):
        left = columns[:, 2 * pair : 2 * pair + 1]
        right = columns[:, 2 * pair + 1 : 2 * pair + 2]
        parts.append(jnp.where(lower, left, right))
    return jnp.concatenate(parts, axis=1)


def lower_lanes(rows):
    return lax.broadcasted_iota(jnp.int32, (rows, 128), 1) < HDIM


def head_sums(values):
    width = values.shape[1]
    row = lax.broadcasted_iota(jnp.int32, (width, width // HDIM), 0)
    column = lax.broadcasted_iota(jnp.int32, (width, width // HDIM), 1)
    ones = ((row >= column * HDIM) & (row < (column + 1) * HDIM)).astype(F32).astype(BF16)
    return dot2(values, ones, 1, 0)


def params():
    return pltpu.CompilerParams(vmem_limit_bytes=40 * 1024 * 1024)


def prompt_state_body(x_ref, b_ref, w_ref, out_ref):
    step = pl.program_id(0)
    weighted = spread(w_ref[0], lower_lanes(x_ref.shape[0])) * x_ref[...].astype(F32)
    hi, lo = split(weighted)
    result = dot(b_ref[...], hi, 0, 0) + dot(b_ref[...], lo, 0, 0)

    @pl.when(step == 0)
    def _():
        out_ref[...] = result

    @pl.when(step > 0)
    def _():
        out_ref[...] += result


def prompt_state(x, b, w, group):
    width = x.shape[1] // 2
    rows = 128
    return pl.pallas_call(
        prompt_state_body,
        grid=(LP // rows,),
        in_specs=[
            pl.BlockSpec((rows, width), lambda i: (i, group)),
            pl.BlockSpec((rows, STATE), lambda i: (i, group)),
            pl.BlockSpec((1, rows, width // HDIM), lambda i: (group, i, 0)),
        ],
        out_specs=pl.BlockSpec((STATE, width), lambda i: (0, 0)),
        out_shape=jax.ShapeDtypeStruct((STATE, width), F32),
        compiler_params=params(),
        name="prompt_state",
    )(x, b, w)


def pick(offset, one, two, three):
    return jnp.where(offset == 1, one, jnp.where(offset == 2, two, three))


def attention_body(
    meta, q_ref, cot_ref, k_ref, v_ref, kv1, k2, v2, kv3,
    out_ref, gq_ref, gk_ref, gv_ref, g1, gk2, gv2, g3,
):
    reply = pl.program_id(1)
    offset = meta[reply]
    length = meta[2 + reply]
    given = pick(offset, kv1[: MARK + LP], k2[...], kv3[: MARK + LP])
    prior = jnp.concatenate([given[0:1]] * ((LP + LR) // AHDIM), axis=1).astype(jnp.int32)
    keys = jnp.concatenate([given[MARK:].astype(BF16), k_ref[0]], axis=0)
    given = pick(offset, kv1[MARK + LP :], v2[...], kv3[MARK + LP :])
    values = jnp.concatenate([given.astype(BF16), v_ref[0]], axis=0)
    scale = AHDIM ** (-0.5)
    heads = 2
    rows = heads * LR
    total = LP + LR
    token = lax.broadcasted_iota(jnp.int32, (rows, total), 0) % LR
    key = lax.broadcasted_iota(jnp.int32, (rows, total), 1)
    own = key - LP
    allowed = ((key < LP) & (key < prior)) | ((own >= 0) & (own <= token) & (own < length))
    live = (lax.broadcasted_iota(jnp.int32, (rows, AHDIM), 0) % LR < length).astype(F32)
    grad_keys = jnp.zeros((total, AHDIM), F32)
    grad_values = jnp.zeros((total, AHDIM), F32)
    for part in range(8 // heads):
        lanes = [slice((part * heads + i) * AHDIM, (part * heads + i + 1) * AHDIM) for i in range(heads)]
        query = jnp.concatenate([q_ref[0, :, at] for at in lanes], axis=0)
        grad_out = jnp.concatenate([cot_ref[0, :, at] for at in lanes], axis=0)
        grad_out = (grad_out.astype(F32) * live).astype(BF16)
        scores = jnp.where(allowed, dot(query, keys, 1, 1) * scale, -1e30)
        top = jnp.max(scores, axis=1, keepdims=True)
        weights = jnp.exp(scores - top)
        weights = weights * (1.0 / jnp.sum(weights, axis=1, keepdims=True))
        weights_hi, weights_lo = split(weights)
        out = dot(weights_hi, values, 1, 0) + dot(weights_lo, values, 1, 0)
        inner = jnp.sum(out * grad_out.astype(F32), axis=1, keepdims=True)
        grad_scores = weights * (dot(grad_out, values, 1, 1) - inner) * scale
        grad_hi, grad_lo = split(grad_scores)
        grad_query = dot(grad_hi, keys, 1, 0) + dot(grad_lo, keys, 1, 0)
        grad_keys += dot(grad_hi, query, 0, 0) + dot(grad_lo, query, 0, 0)
        grad_values += dot(weights_hi, grad_out, 0, 0) + dot(weights_lo, grad_out, 0, 0)
        out = out * live
        for i, at in enumerate(lanes):
            out_ref[0, :, at] = out[i * LR : (i + 1) * LR].astype(BF16)
            gq_ref[0, :, at] = grad_query[i * LR : (i + 1) * LR].astype(BF16)
    gk_ref[0] = grad_keys[LP:].astype(BF16)
    gv_ref[0] = grad_values[LP:].astype(BF16)
    for number, (key_out, value_out) in enumerate(((g1, g1), (gk2, gv2), (g3, g3))):
        share = (offset == number + 1).astype(F32)
        key_rows = pl.ds(0, LP)
        value_rows = pl.ds(value_out.shape[0] - LP, LP)

        @pl.when(reply == 0)
        def _():
            key_out[key_rows] = grad_keys[:LP] * share
            value_out[value_rows] = grad_values[:LP] * share

        @pl.when(reply > 0)
        def _():
            key_out[key_rows] += grad_keys[:LP] * share
            value_out[value_rows] += grad_values[:LP] * share


def attention(meta, q, cot, k, v, one, two, three):
    replies, length, width = q.shape
    kv_heads = k.shape[2] // AHDIM
    wide = width // kv_heads
    by_reply = lambda size: pl.BlockSpec((1, length, size), lambda h, r, m: (r, 0, h))
    prior = lambda rows: pl.BlockSpec((rows, AHDIM), lambda h, r, m: (0, h))
    prior_shape = lambda rows: jax.ShapeDtypeStruct((rows, k.shape[2]), F32)
    out_rows = (2 * LP, LP, LP, 2 * LP)
    outs = pl.pallas_call(
        attention_body,
        grid_spec=pltpu.PrefetchScalarGridSpec(
            num_scalar_prefetch=1,
            grid=(kv_heads, replies),
            in_specs=[by_reply(wide), by_reply(wide), by_reply(AHDIM), by_reply(AHDIM)]
            + [prior(MARK + 2 * LP), prior(MARK + LP), prior(LP), prior(MARK + 2 * LP)],
            out_specs=[by_reply(wide), by_reply(wide), by_reply(AHDIM), by_reply(AHDIM)]
            + [prior(rows) for rows in out_rows],
        ),
        out_shape=[
            jax.ShapeDtypeStruct(q.shape, BF16),
            jax.ShapeDtypeStruct(q.shape, BF16),
            jax.ShapeDtypeStruct(k.shape, BF16),
            jax.ShapeDtypeStruct(k.shape, BF16),
        ]
        + [prior_shape(rows) for rows in out_rows],
        compiler_params=params(),
        name="attention",
    )(meta, q, cot, k, v, one, *two, three)
    return outs[:4], (outs[4], outs[5:7], outs[7])


def carried_state(offset, one, two_upper, two_lower, three):
    two = jnp.concatenate([two_upper[...], two_lower[...]], axis=0)
    return split(pick(offset, one[...], two, three[...]))


def ssm_forward_body(
    meta, x_ref, cot_ref, gain_ref, b_ref, c_ref, decay_t, fade_t, source,
    s1, s2a, s2b, s3, before_ref, raw_ref, sums_ref,
):
    reply = pl.program_id(0)
    length = meta[2 + reply]
    state = carried_state(meta[reply], s1, s2a, s2b, s3)
    c = c_ref[0]
    meeting = dot(c, b_ref[0], 1, 1)
    causal = lax.broadcasted_iota(jnp.int32, (LR, LR), 0) >= lax.broadcasted_iota(jnp.int32, (LR, LR), 1)
    lower = lower_lanes(LR)
    live = (lax.broadcasted_iota(jnp.int32, (LR, 128), 0) < length).astype(F32)
    carried = dot(c, state[0], 1, 0) + dot(c, state[1], 1, 0)
    decay = decay_t[0, 0]
    fade = fade_t[0, 0]
    squares = jnp.zeros((LR, 128), F32)
    inner = jnp.zeros((LR, 128), F32)
    for pair in range(x_ref.shape[2] // 128):
        lanes = slice(pair * 128, (pair + 1) * 128)
        mixing = []
        for head in (2 * pair, 2 * pair + 1):
            exponent = decay[:, head : head + 1] - source[0, head : head + 1, :]
            mixing.append(jnp.exp(jnp.where(causal, exponent, -1e30)) * meeting)
        both = dot2(jnp.concatenate(mixing, axis=0), x_ref[0, :, lanes], 1, 0)
        local = jnp.where(lower, both[:LR], both[LR:])
        fading = jnp.where(lower, fade[:, 2 * pair : 2 * pair + 1], fade[:, 2 * pair + 1 : 2 * pair + 2])
        raw = (local + carried[:, lanes] * fading) * live
        raw_ref[0, :, lanes] = raw
        squares += raw * raw
        inner += cot_ref[0, :, lanes].astype(F32) * gain_ref[:, lanes] * raw
    ones = jnp.ones((8, 128), BF16)
    for row, partial in enumerate((squares, inner)):
        hi, lo = split(partial)
        sums_ref[0, row : row + 1, :] = (dot(ones, hi, 1, 1) + dot(ones, lo, 1, 1))[0:1] + before_ref[0, row : row + 1, :]


def state_specs(width):
    return [pl.BlockSpec((rows, width), lambda r, m: (0, 0)) for rows in (STATE, STATE // 2, STATE // 2, STATE)]


def ssm_forward(meta, x, cot, gain, b, c, decay_t, fade_t, source, states, before, group):
    replies, length, width = x.shape
    width //= 2
    heads = width // HDIM
    wide = pl.BlockSpec((1, length, width), lambda r, m: (r, 0, group))
    thin = pl.BlockSpec((1, length, STATE), lambda r, m: (r, 0, group))
    columns = pl.BlockSpec((1, 1, length, heads), lambda r, m: (r, group, 0, 0))
    sums = pl.BlockSpec((1, 2, length), lambda r, m: (r, 0, 0))
    return pl.pallas_call(
        ssm_forward_body,
        grid_spec=pltpu.PrefetchScalarGridSpec(
            num_scalar_prefetch=1,
            grid=(replies,),
            in_specs=[
                wide,
                wide,
                pl.BlockSpec((1, width), lambda r, m: (0, group)),
                thin,
                thin,
                columns,
                columns,
                pl.BlockSpec((1, heads, length), lambda r, m: (r, group, 0)),
            ]
            + state_specs(width)
            + [sums],
            out_specs=[pl.BlockSpec((1, length, width), lambda r, m: (r, 0, 0)), sums],
        ),
        out_shape=[
            jax.ShapeDtypeStruct((replies, length, width), F32),
            jax.ShapeDtypeStruct((replies, 2, length), F32),
        ],
        compiler_params=params(),
        name="ssm_forward",
    )(meta, x, cot, gain, b, c, decay_t, fade_t, source, *states, before)


def ssm_backward_body(
    meta, raw_ref, x_ref, cot_ref, gain_ref, b_ref, c_ref, norm_ref, fade_t, source_t, decay,
    s1, s2a, s2b, s3, *rest,
):
    out_ref, gx_ref, gb_ref, gc_ref, rows_ref, columns_ref, g1, g2a, g2b, g3 = rest[-10:]
    reply = pl.program_id(0)
    offset = meta[reply]
    length = meta[2 + reply]
    state = carried_state(offset, s1, s2a, s2b, s3)
    b = b_ref[0]
    c = c_ref[0]
    meeting = dot(b, c, 1, 1)
    later = lax.broadcasted_iota(jnp.int32, (LR, LR), 1) >= lax.broadcasted_iota(jnp.int32, (LR, LR), 0)
    lower = lower_lanes(LR)
    live = (lax.broadcasted_iota(jnp.int32, (LR, 128), 0) < length).astype(F32)
    features = HEADS * HDIM
    diagonal = lax.broadcasted_iota(jnp.int32, (LR, LR), 1) == lax.broadcasted_iota(jnp.int32, (LR, LR), 0)
    squares = jnp.sum(jnp.where(diagonal, norm_ref[0, 0:1, :], 0.0), axis=1, keepdims=True)
    inner = jnp.sum(jnp.where(diagonal, norm_ref[0, 1:2, :], 0.0), axis=1, keepdims=True)
    factor = lax.rsqrt(squares / features + 1e-05)
    scaled = factor * factor * factor * inner / features
    fade = fade_t[0, 0]
    source = source_t[0, 0]
    grad_meeting = jnp.zeros((LR, LR), F32)
    row_parts = []
    column_parts = []
    faded = []
    for pair in range(x_ref.shape[2] // 128):
        lanes = slice(pair * 128, (pair + 1) * 128)
        raw = raw_ref[0, :, lanes]
        gain = gain_ref[:, lanes]
        out_ref[0, :, lanes] = (raw * factor * gain).astype(BF16)
        grad = (factor * (cot_ref[0, :, lanes].astype(F32) * gain) - raw * scaled) * live
        grad_pair = split(grad)
        x = x_ref[0, :, lanes]
        zero = jnp.zeros_like(x)
        x_both = jnp.concatenate([jnp.where(lower, x, zero), jnp.where(lower, zero, x)], axis=0)
        grad_mixing = dot(x_both, grad_pair[0], 1, 1) + dot(x_both, grad_pair[1], 1, 1)
        mixing = []
        for i in range(2):
            head = 2 * pair + i
            exponent = decay[0, head : head + 1, :] - source[:, head : head + 1]
            table = jnp.exp(jnp.where(later, exponent, -1e30))
            grad_meeting += grad_mixing[i * LR : (i + 1) * LR] * table
            mixing.append(table * meeting)
        both = dot3(split(jnp.concatenate(mixing, axis=0)), grad_pair, 1, 0)
        grad_x = jnp.where(lower, both[:LR], both[LR:])
        gx_ref[0, :, lanes] = grad_x.astype(BF16)
        row_parts.append(grad * raw)
        column_parts.append(grad_x * x.astype(F32))
        fading = jnp.where(lower, fade[:, 2 * pair : 2 * pair + 1], fade[:, 2 * pair + 1 : 2 * pair + 2])
        faded.append(grad * fading)
    rows_ref[0] = head_sums(jnp.concatenate(row_parts, axis=1))
    columns_ref[0] = head_sums(jnp.concatenate(column_parts, axis=1))
    faded = split(jnp.concatenate(faded, axis=1))
    meeting_pair = split(grad_meeting)
    gb_ref[0] = (dot(meeting_pair[0], c, 1, 0) + dot(meeting_pair[1], c, 1, 0)).astype(BF16)
    grad_c = dot(meeting_pair[0], b, 0, 0) + dot(meeting_pair[1], b, 0, 0)
    gc_ref[0] = (grad_c + dot3(faded, state, 1, 1)).astype(BF16)
    grad_state = dot(c, faded[0], 0, 0) + dot(c, faded[1], 0, 0)
    for number, (upper_out, lower_out) in enumerate(((g1, g1), (g2a, g2b), (g3, g3))):
        share = (offset == number + 1).astype(F32)
        upper = pl.ds(0, STATE // 2)
        lower = pl.ds(lower_out.shape[0] - STATE // 2, STATE // 2)

        @pl.when(reply == 0)
        def _():
            upper_out[upper] = grad_state[: STATE // 2] * share
            lower_out[lower] = grad_state[STATE // 2 :] * share

        @pl.when(reply > 0)
        def _():
            upper_out[upper] += grad_state[: STATE // 2] * share
            lower_out[lower] += grad_state[STATE // 2 :] * share


def ssm_backward(meta, raw, x, cot, gain, b, c, norm, fade_t, source_t, decay, states, group, before):
    replies, length, full = x.shape
    width = full // 2
    heads = width // HDIM
    wide = pl.BlockSpec((1, length, width), lambda r, m: (r, 0, group))
    own = pl.BlockSpec((1, length, width), lambda r, m: (r, 0, 0))
    thin = pl.BlockSpec((1, length, STATE), lambda r, m: (r, 0, group))
    columns = pl.BlockSpec((1, 1, length, heads), lambda r, m: (r, group, 0, 0))
    sums = pl.BlockSpec((1, length, heads), lambda r, m: (r, 0, 0))
    inputs = [raw, x, cot, gain, b, c, norm, fade_t, source_t, decay, *states]
    in_specs = [
        own,
        wide,
        wide,
        pl.BlockSpec((1, width), lambda r, m: (0, group)),
        thin,
        thin,
        pl.BlockSpec((1, 2, length), lambda r, m: (r, 0, 0)),
        columns,
        columns,
        pl.BlockSpec((1, heads, length), lambda r, m: (r, group, 0)),
    ] + state_specs(width)
    aliases = {}
    if before is not None:
        aliases = {1 + len(inputs) + i: i for i in range(4)}
        inputs += before
        in_specs += [pl.BlockSpec(memory_space=pl.ANY)] * 4
    whole = jax.ShapeDtypeStruct((STATE, width), F32)
    half = jax.ShapeDtypeStruct((STATE // 2, width), F32)
    outs = pl.pallas_call(
        ssm_backward_body,
        grid_spec=pltpu.PrefetchScalarGridSpec(
            num_scalar_prefetch=1,
            grid=(replies,),
            in_specs=in_specs,
            out_specs=[wide, wide, thin, thin, sums, sums] + state_specs(width),
        ),
        out_shape=[
            jax.ShapeDtypeStruct(x.shape, BF16),
            jax.ShapeDtypeStruct(x.shape, BF16),
            jax.ShapeDtypeStruct(b.shape, BF16),
            jax.ShapeDtypeStruct(b.shape, BF16),
            jax.ShapeDtypeStruct((replies, length, heads), F32),
            jax.ShapeDtypeStruct((replies, length, heads), F32),
        ]
        + [whole, half, half, whole],
        input_output_aliases=aliases,
        compiler_params=params(),
        name="ssm_backward",
    )(meta, *inputs)
    return outs[:4], outs[4], outs[5], (outs[6], outs[7:9], outs[9])


def prompt_grad_body(x_ref, b_ref, w_ref, grad_ref, *rest):
    gx_ref, gmap_ref, sums_ref = rest[-3:]
    grad = split(grad_ref[...])
    x = x_ref[...].astype(F32)
    weight = spread(w_ref[0], lower_lanes(x.shape[0]))
    b = b_ref[...]
    pulled = dot(b, grad[0], 1, 0) + dot(b, grad[1], 1, 0)
    gx_ref[...] = (weight * pulled).astype(BF16)
    gmap_ref[...] = dot3(split(weight * x), grad, 1, 1).astype(BF16)
    sums_ref[...] = head_sums(x * pulled)


def prompt_grad(x, b, w, grad, group, before):
    width = x.shape[1] // 2
    heads = width // HDIM
    rows = 128
    inputs = [x, b, w, grad]
    in_specs = [
        pl.BlockSpec((rows, width), lambda i: (i, group)),
        pl.BlockSpec((rows, STATE), lambda i: (i, group)),
        pl.BlockSpec((1, rows, heads), lambda i: (group, i, 0)),
        pl.BlockSpec((STATE, width), lambda i: (0, 0)),
    ]
    aliases = {}
    if before is not None:
        aliases = {len(inputs) + i: i for i in range(2)}
        inputs += before
        in_specs += [pl.BlockSpec(memory_space=pl.ANY)] * 2
    outs = pl.pallas_call(
        prompt_grad_body,
        grid=(LP // rows,),
        in_specs=in_specs,
        out_specs=[
            pl.BlockSpec((rows, width), lambda i: (i, group)),
            pl.BlockSpec((rows, STATE), lambda i: (i, group)),
            pl.BlockSpec((rows, heads), lambda i: (i, 0)),
        ],
        out_shape=[
            jax.ShapeDtypeStruct(x.shape, BF16),
            jax.ShapeDtypeStruct(b.shape, BF16),
            jax.ShapeDtypeStruct((LP, heads), F32),
        ],
        input_output_aliases=aliases,
        compiler_params=params(),
        name="prompt_grad",
    )(*inputs)
    return outs[:2], outs[2]


def tables(count):
    last = ROW - 1
    across = [(i, (i + ROW) % count) for i in range(count) if i % ROW == last]
    ahead = [(i, i + 1 if i % ROW != last else i - last) for i in range(count)]
    behind = [(i, (i + last) % count if i % ROW != last else i - 1) for i in range(count)]
    forward = [(i, (i + 1) % count) for i in range(count)]
    return across, ahead, behind, forward


def turned(pairs):
    return [(b, a) for a, b in pairs]


def move(part, pairs):
    return lax.ppermute(part, "seq", pairs)


def merge(part, moved, is_last):
    return jnp.where(is_last, 0.0, part) + moved


def together(*values):
    return lax.optimization_barrier(values)


def columns_of(rows):
    heads, tokens = rows.shape[-2:]
    cut = rows.reshape(rows.shape[:-2] + (2, heads // 2, tokens))
    return jnp.swapaxes(cut, -1, -2)


def shards(
    prompt_x,
    prompt_b,
    prompt_dt,
    prompt_keys,
    prompt_values,
    prompt_len,
    reply_x,
    reply_b,
    reply_c,
    reply_dt,
    reply_queries,
    reply_keys,
    reply_values,
    reply_len,
    reply_owner,
    decay_log,
    step_bias,
    norm_gain,
    ssm_cotangent,
    attn_cotangent,
):
    seq_count = lax.axis_size("seq")
    position = lax.axis_index("seq")
    pairs = tables(seq_count)
    is_last = position % ROW == ROW - 1

    across, ahead, behind, forward = pairs
    backward = turned(forward)
    keys = prompt_keys[0].astype(F32)
    mark = jnp.full((MARK, keys.shape[1]), prompt_len[0].astype(F32))
    own = jnp.concatenate([mark, keys, prompt_values[0].astype(F32)], axis=0)
    own_moved = move(own, across)

    rate = -jnp.exp(decay_log)
    tokens = jnp.arange(LP)
    prompt_raw = prompt_dt[0].astype(F32) + step_bias[:, None]
    prompt_plus = jax.nn.softplus(prompt_raw)
    prompt_valid = (tokens < prompt_len[0]).astype(F32)[None, :]
    prompt_steps = prompt_plus * prompt_valid
    after = (tokens[:, None] > tokens[None, :]).astype(F32)
    remaining = jnp.einsum("hu,us->hs", prompt_steps, after, precision=HIGHEST)
    weight = prompt_steps * jnp.exp(rate[:, None] * remaining)
    weight_t = columns_of(weight)
    state = [prompt_state(prompt_x[0], prompt_b[0], weight_t, group) for group in range(2)]

    times = jnp.arange(LR)
    reply_raw = reply_dt.astype(F32) + step_bias[None, :, None]
    reply_plus = jax.nn.softplus(reply_raw)
    reply_valid = (times[None, :] < reply_len[:, None])[:, None, :]
    reply_steps = jnp.where(reply_valid, reply_plus, 0.0)
    until = (times[:, None] <= times[None, :]).astype(F32)
    running = jnp.einsum("rhu,ut->rht", reply_steps, until, precision=HIGHEST)
    decay = rate[None, :, None] * running
    source = decay - jnp.where(reply_valid, jnp.log(reply_plus), -1e30)
    decay_t = columns_of(decay)
    fade_t = jnp.exp(decay_t)
    source_t = columns_of(source)

    offsets = (position - reply_owner) % seq_count
    meta = jnp.concatenate([offsets, reply_len]).astype(jnp.int32)

    gain = norm_gain[None, :]
    key_cut = MARK + LP
    cut = STATE // 2

    def spread_out(one, three, at):
        return move(one[:at], forward), move(three[at:], backward)

    def gather_in(parts):
        return move(parts[1][0], backward), move(parts[1][1], forward)

    def homeward(parts, came):
        at = came[0].shape[0]
        one = jnp.concatenate([parts[0][:at] + came[0], parts[0][at:]], axis=0)
        three = jnp.concatenate([parts[2][:at], parts[2][at:] + came[1]], axis=0)
        return move(one, turned(ahead)), move(three, turned(behind))

    own = merge(own, own_moved, is_last)
    own, first = together(own, state[0])
    own_one, own_three = move(own, ahead), move(own, behind)
    first_moved = move(first, across)

    first = merge(first, first_moved, is_last)
    own_one, own_three, first, second = together(own_one, own_three, first, state[1])
    own_two = spread_out(own_one, own_three, key_cut)
    first_one, first_three = move(first, ahead), move(first, behind)
    second_moved = move(second, across)

    second = merge(second, second_moved, is_last)
    own_two, first_one, first_three, second, queries = together(
        own_two, first_one, first_three, second, reply_queries
    )
    first_two = spread_out(first_one, first_three, cut)
    second_one, second_three = move(second, ahead), move(second, behind)
    (attn_output, grad_queries, grad_keys, grad_values), own_parts = attention(
        meta, queries, attn_cotangent, reply_keys, reply_values, own_one, own_two, own_three
    )

    first_two, second_one, second_three, own_parts, x = together(
        first_two, second_one, second_three, own_parts, reply_x
    )
    second_two = spread_out(second_one, second_three, cut)
    states = [(first_one, *first_two, first_three), (second_one, *second_two, second_three)]

    def forward_part(group, x, before):
        return ssm_forward(
            meta, x, ssm_cotangent, gain, reply_b, reply_c, decay_t, fade_t, source, states[group], before, group
        )

    def backward_part(group, raw, before):
        return ssm_backward(
            meta, raw, reply_x, ssm_cotangent, gain, reply_b, reply_c, sums, fade_t, source_t, decay,
            states[group], group, before,
        )

    raw_first, sums = forward_part(0, x, jnp.zeros((reply_x.shape[0], 2, LR), F32))

    states[1], own_parts, x = together(states[1], own_parts, x)
    own_came = gather_in(own_parts)
    raw_second, sums = forward_part(1, x, sums)
    sums = lax.psum(sums, "head")
    wide, rows_first, columns_first, first_parts = backward_part(0, raw_first, None)
    own_home = homeward(own_parts, own_came)

    own_home, first_parts, raw_second = together(own_home, first_parts, raw_second)
    first_came = gather_in(first_parts)
    wide, rows_second, columns_second, second_parts = backward_part(1, raw_second, wide)
    ssm_output, grad_x, grad_b, grad_c = wide
    rows = [rows_first, rows_second]
    columns = [columns_first, columns_second]

    first_came, second_parts, own_home = together(first_came, second_parts, own_home)
    first_home = homeward(first_parts, first_came)
    second_came = gather_in(second_parts)
    own_total = own_home[0] + own_home[1]
    own_last = move(own_total, turned(across))

    first_home, second_came, own_last = together(first_home, second_came, own_last)
    own_total = merge(own_total, own_last, is_last)
    grad_prompt_keys, grad_prompt_values = own_total[:LP], own_total[LP:]
    second_home = homeward(second_parts, second_came)
    first_total = first_home[0] + first_home[1]
    first_last = move(first_total, turned(across))

    second_total = second_home[0] + second_home[1]
    second_last = move(second_total, turned(across))
    grads = [merge(first_total, first_last, is_last), merge(second_total, second_last, is_last)]

    rows = jnp.concatenate(rows, axis=-1)
    columns = jnp.concatenate(columns, axis=-1)
    grad_running = rate * (rows - columns)
    grad_steps = jnp.einsum("rth,ut->rhu", grad_running, until, precision=HIGHEST)
    grad_steps += jnp.swapaxes(columns, 1, 2) / reply_plus
    grad_reply_dt = jnp.where(reply_valid, grad_steps * jax.nn.sigmoid(reply_raw), 0.0).astype(BF16)

    wide = None
    shares = []
    for group in range(2):
        wide, share = prompt_grad(prompt_x[0], prompt_b[0], weight_t, grads[group], group, wide)
        shares.append(share)
    grad_px, grad_pb = wide
    share = jnp.concatenate(shares, axis=-1).T * weight
    earlier = jnp.einsum("hs,su->hu", share, after.T, precision=HIGHEST)
    grad_prompt_steps = share / prompt_plus + rate[:, None] * earlier
    grad_prompt_dt = (grad_prompt_steps * prompt_valid * jax.nn.sigmoid(prompt_raw)).astype(BF16)

    return (
        ssm_output,
        attn_output,
        grad_x,
        grad_b,
        grad_c,
        grad_reply_dt,
        grad_queries,
        grad_keys,
        grad_values,
        grad_px[None],
        grad_pb[None],
        grad_prompt_dt[None],
        grad_prompt_keys.astype(BF16)[None],
        grad_prompt_values.astype(BF16)[None],
    )


def solution(mesh):
    placed = (
        P("seq", None, "head"),
        P("seq", None, "head"),
        P("seq", "head", None),
        P("seq", None, "head"),
        P("seq", None, "head"),
        P("seq"),
        P("seq", None, "head"),
        P("seq", None, "head"),
        P("seq", None, "head"),
        P("seq", "head", None),
        P("seq", None, "head"),
        P("seq", None, "head"),
        P("seq", None, "head"),
        P("seq"),
        P("seq"),
        P("head"),
        P("head"),
        P("head"),
        P("seq", None, "head"),
        P("seq", None, "head"),
    )
    return jax.shard_map(
        shards,
        mesh=mesh,
        in_specs=placed,
        out_specs=(
            P("seq", None, "head"),
            P("seq", None, "head"),
            P("seq", None, "head"),
            P("seq", None, "head"),
            P("seq", None, "head"),
            P("seq", "head", None),
            P("seq", None, "head"),
            P("seq", None, "head"),
            P("seq", None, "head"),
            P("seq", None, "head"),
            P("seq", None, "head"),
            P("seq", "head", None),
            P("seq", None, "head"),
            P("seq", None, "head"),
        ),
        check_vma=False,
    )
```

```python
import jax
import jax.numpy as jnp
from jax import lax
from jax.experimental import pallas as pl
from jax.experimental.pallas import tpu as pltpu
from jax.sharding import PartitionSpec as P

HEADS = 128
HDIM = 64
STATE = 128
AHDIM = 128
OFFSETS = 3
LP = 512
LR = 128
MARK = 8
ROW = 4

HIGHEST = lax.Precision.HIGHEST
F32 = jnp.float32
BF16 = jnp.bfloat16


def split(a):
    hi = a.astype(BF16)
    return hi, (a - hi.astype(F32)).astype(BF16)


def dot(a, b, ca, cb):
    return lax.dot_general(a, b, (((ca,), (cb,)), ((), ())), preferred_element_type=F32)


def dot2(a, b, ca, cb):
    hi, lo = split(a)
    return dot(hi, b, ca, cb) + dot(lo, b, ca, cb)


def dot3(a, b, ca, cb):
    return dot(a[0], b[0], ca, cb) + (dot(a[1], b[0], ca, cb) + dot(a[0], b[1], ca, cb))


def spread(columns, lower):
    parts = []
    for pair in range(columns.shape[1] // 2):
        left = columns[:, 2 * pair : 2 * pair + 1]
        right = columns[:, 2 * pair + 1 : 2 * pair + 2]
        parts.append(jnp.where(lower, left, right))
    return jnp.concatenate(parts, axis=1)


def lower_lanes(rows):
    return lax.broadcasted_iota(jnp.int32, (rows, 128), 1) < HDIM


def head_sums(values):
    width = values.shape[1]
    row = lax.broadcasted_iota(jnp.int32, (width, width // HDIM), 0)
    column = lax.broadcasted_iota(jnp.int32, (width, width // HDIM), 1)
    ones = ((row >= column * HDIM) & (row < (column + 1) * HDIM)).astype(F32).astype(BF16)
    return dot2(values, ones, 1, 0)


def params(mebibytes):
    return pltpu.CompilerParams(vmem_limit_bytes=mebibytes * 1024 * 1024)


def prompt_state_body(x_ref, b_ref, w_ref, out_ref):
    step = pl.program_id(0)
    weighted = spread(w_ref[0], lower_lanes(x_ref.shape[0])) * x_ref[...].astype(F32)
    hi, lo = split(weighted)
    result = dot(b_ref[...], hi, 0, 0) + dot(b_ref[...], lo, 0, 0)

    @pl.when(step == 0)
    def _():
        out_ref[...] = result

    @pl.when(step > 0)
    def _():
        out_ref[...] += result


def prompt_state(x, b, w, group):
    width = x.shape[1] // 2
    rows = 256
    return pl.pallas_call(
        prompt_state_body,
        grid=(LP // rows,),
        in_specs=[
            pl.BlockSpec((rows, width), lambda i: (i, group)),
            pl.BlockSpec((rows, STATE), lambda i: (i, group)),
            pl.BlockSpec((1, rows, width // HDIM), lambda i: (group, i, 0)),
        ],
        out_specs=pl.BlockSpec((STATE, width), lambda i: (0, 0)),
        out_shape=jax.ShapeDtypeStruct((STATE, width), F32),
        compiler_params=params(40),
        name="prompt_state",
    )(x, b, w)


def pick(offset, one, two, three):
    return jnp.where(offset == 1, one, jnp.where(offset == 2, two, three))


def attention_body(
    meta, q_ref, cot_ref, k_ref, v_ref, kv1, k2, v2, kv3,
    out_ref, gq_ref, gk_ref, gv_ref, g1, gk2, gv2, g3,
):
    reply = pl.program_id(1)
    offset = meta[reply]
    length = meta[2 + reply]
    given = pick(offset, kv1[: MARK + LP], k2[...], kv3[: MARK + LP])
    prior = jnp.concatenate([given[0:1]] * ((LP + LR) // AHDIM), axis=1).astype(jnp.int32)
    keys = jnp.concatenate([given[MARK:].astype(BF16), k_ref[0]], axis=0)
    given = pick(offset, kv1[MARK + LP :], v2[...], kv3[MARK + LP :])
    values = jnp.concatenate([given.astype(BF16), v_ref[0]], axis=0)
    scale = AHDIM ** (-0.5)
    heads = 2
    rows = heads * LR
    total = LP + LR
    token = lax.broadcasted_iota(jnp.int32, (rows, total), 0) % LR
    key = lax.broadcasted_iota(jnp.int32, (rows, total), 1)
    own = key - LP
    allowed = ((key < LP) & (key < prior)) | ((own >= 0) & (own <= token) & (own < length))
    live = (lax.broadcasted_iota(jnp.int32, (rows, AHDIM), 0) % LR < length).astype(F32)
    grad_keys = jnp.zeros((total, AHDIM), F32)
    grad_values = jnp.zeros((total, AHDIM), F32)
    for part in range(8 // heads):
        lanes = [slice((part * heads + i) * AHDIM, (part * heads + i + 1) * AHDIM) for i in range(heads)]
        query = jnp.concatenate([q_ref[0, :, at] for at in lanes], axis=0)
        grad_out = jnp.concatenate([cot_ref[0, :, at] for at in lanes], axis=0)
        grad_out = (grad_out.astype(F32) * live).astype(BF16)
        scores = jnp.where(allowed, dot(query, keys, 1, 1) * scale, -1e30)
        top = jnp.max(scores, axis=1, keepdims=True)
        weights = jnp.exp(scores - top)
        weights = weights * (1.0 / jnp.sum(weights, axis=1, keepdims=True))
        weights_hi, weights_lo = split(weights)
        out = dot(weights_hi, values, 1, 0) + dot(weights_lo, values, 1, 0)
        inner = jnp.sum(out * grad_out.astype(F32), axis=1, keepdims=True)
        grad_scores = weights * (dot(grad_out, values, 1, 1) - inner) * scale
        grad_hi, grad_lo = split(grad_scores)
        grad_query = dot(grad_hi, keys, 1, 0) + dot(grad_lo, keys, 1, 0)
        grad_keys += dot(grad_hi, query, 0, 0) + dot(grad_lo, query, 0, 0)
        grad_values += dot(weights_hi, grad_out, 0, 0) + dot(weights_lo, grad_out, 0, 0)
        out = out * live
        for i, at in enumerate(lanes):
            out_ref[0, :, at] = out[i * LR : (i + 1) * LR].astype(BF16)
            gq_ref[0, :, at] = grad_query[i * LR : (i + 1) * LR].astype(BF16)
    gk_ref[0] = grad_keys[LP:].astype(BF16)
    gv_ref[0] = grad_values[LP:].astype(BF16)
    for number, (key_out, value_out) in enumerate(((g1, g1), (gk2, gv2), (g3, g3))):
        share = (offset == number + 1).astype(F32)
        key_rows = pl.ds(0, LP)
        value_rows = pl.ds(value_out.shape[0] - LP, LP)

        @pl.when(reply == 0)
        def _():
            key_out[key_rows] = grad_keys[:LP] * share
            value_out[value_rows] = grad_values[:LP] * share

        @pl.when(reply > 0)
        def _():
            key_out[key_rows] += grad_keys[:LP] * share
            value_out[value_rows] += grad_values[:LP] * share


def attention(meta, q, cot, k, v, one, two, three):
    replies, length, width = q.shape
    kv_heads = k.shape[2] // AHDIM
    wide = width // kv_heads
    by_reply = lambda size: pl.BlockSpec((1, length, size), lambda h, r, m: (r, 0, h))
    prior = lambda rows: pl.BlockSpec((rows, AHDIM), lambda h, r, m: (0, h))
    prior_shape = lambda rows: jax.ShapeDtypeStruct((rows, k.shape[2]), F32)
    out_rows = (2 * LP, LP, LP, 2 * LP)
    outs = pl.pallas_call(
        attention_body,
        grid_spec=pltpu.PrefetchScalarGridSpec(
            num_scalar_prefetch=1,
            grid=(kv_heads, replies),
            in_specs=[by_reply(wide), by_reply(wide), by_reply(AHDIM), by_reply(AHDIM)]
            + [prior(MARK + 2 * LP), prior(MARK + LP), prior(LP), prior(MARK + 2 * LP)],
            out_specs=[by_reply(wide), by_reply(wide), by_reply(AHDIM), by_reply(AHDIM)]
            + [prior(rows) for rows in out_rows],
        ),
        out_shape=[
            jax.ShapeDtypeStruct(q.shape, BF16),
            jax.ShapeDtypeStruct(q.shape, BF16),
            jax.ShapeDtypeStruct(k.shape, BF16),
            jax.ShapeDtypeStruct(k.shape, BF16),
        ]
        + [prior_shape(rows) for rows in out_rows],
        compiler_params=params(60),
        name="attention",
    )(meta, q, cot, k, v, one, *two, three)
    return outs[:4], (outs[4], outs[5:7], outs[7])


def carried_state(offset, one, two_upper, two_lower, three):
    two = jnp.concatenate([two_upper[...], two_lower[...]], axis=0)
    return split(pick(offset, one[...], two, three[...]))


def ssm_forward_body(
    meta, x_ref, cot_ref, gain_ref, b_ref, c_ref, decay_t, fade_t, source,
    s1, s2a, s2b, s3, before_ref, raw_ref, sums_ref,
):
    reply = pl.program_id(0)
    length = meta[2 + reply]
    state = carried_state(meta[reply], s1, s2a, s2b, s3)
    c = c_ref[0]
    meeting = dot(c, b_ref[0], 1, 1)
    causal = lax.broadcasted_iota(jnp.int32, (LR, LR), 0) >= lax.broadcasted_iota(jnp.int32, (LR, LR), 1)
    lower = lower_lanes(LR)
    live = (lax.broadcasted_iota(jnp.int32, (LR, 128), 0) < length).astype(F32)
    carried = dot(c, state[0], 1, 0) + dot(c, state[1], 1, 0)
    decay = decay_t[0, 0]
    fade = fade_t[0, 0]
    squares = jnp.zeros((LR, 128), F32)
    inner = jnp.zeros((LR, 128), F32)
    for pair in range(x_ref.shape[2] // 128):
        lanes = slice(pair * 128, (pair + 1) * 128)
        mixing = []
        for head in (2 * pair, 2 * pair + 1):
            exponent = decay[:, head : head + 1] - source[0, head : head + 1, :]
            mixing.append(jnp.exp(jnp.where(causal, exponent, -1e30)) * meeting)
        both = dot2(jnp.concatenate(mixing, axis=0), x_ref[0, :, lanes], 1, 0)
        local = jnp.where(lower, both[:LR], both[LR:])
        fading = jnp.where(lower, fade[:, 2 * pair : 2 * pair + 1], fade[:, 2 * pair + 1 : 2 * pair + 2])
        raw = (local + carried[:, lanes] * fading) * live
        raw_ref[0, :, lanes] = raw
        squares += raw * raw
        inner += cot_ref[0, :, lanes].astype(F32) * gain_ref[:, lanes] * raw
    ones = jnp.ones((8, 128), BF16)
    for row, partial in enumerate((squares, inner)):
        hi, lo = split(partial)
        sums_ref[0, row : row + 1, :] = (dot(ones, hi, 1, 1) + dot(ones, lo, 1, 1))[0:1] + before_ref[0, row : row + 1, :]


def state_specs(width):
    return [pl.BlockSpec((rows, width), lambda r, m: (0, 0)) for rows in (STATE, STATE // 2, STATE // 2, STATE)]


def ssm_forward(meta, x, cot, gain, b, c, decay_t, fade_t, source, states, before, group):
    replies, length, width = x.shape
    width //= 2
    heads = width // HDIM
    wide = pl.BlockSpec((1, length, width), lambda r, m: (r, 0, group))
    thin = pl.BlockSpec((1, length, STATE), lambda r, m: (r, 0, group))
    columns = pl.BlockSpec((1, 1, length, heads), lambda r, m: (r, group, 0, 0))
    sums = pl.BlockSpec((1, 2, length), lambda r, m: (r, 0, 0))
    return pl.pallas_call(
        ssm_forward_body,
        grid_spec=pltpu.PrefetchScalarGridSpec(
            num_scalar_prefetch=1,
            grid=(replies,),
            in_specs=[
                wide,
                wide,
                pl.BlockSpec((1, width), lambda r, m: (0, group)),
                thin,
                thin,
                columns,
                columns,
                pl.BlockSpec((1, heads, length), lambda r, m: (r, group, 0)),
            ]
            + state_specs(width)
            + [sums],
            out_specs=[pl.BlockSpec((1, length, width), lambda r, m: (r, 0, 0)), sums],
        ),
        out_shape=[
            jax.ShapeDtypeStruct((replies, length, width), F32),
            jax.ShapeDtypeStruct((replies, 2, length), F32),
        ],
        compiler_params=params(60),
        name="ssm_forward",
    )(meta, x, cot, gain, b, c, decay_t, fade_t, source, *states, before)


def ssm_backward_body(
    meta, raw_ref, x_ref, cot_ref, gain_ref, b_ref, c_ref, norm_ref, fade_t, source_t, decay,
    s1, s2a, s2b, s3, *rest,
):
    out_ref, gx_ref, gb_ref, gc_ref, rows_ref, columns_ref, g1, g2a, g2b, g3 = rest[-10:]
    reply = pl.program_id(0)
    offset = meta[reply]
    length = meta[2 + reply]
    state = carried_state(offset, s1, s2a, s2b, s3)
    b = b_ref[0]
    c = c_ref[0]
    meeting = dot(b, c, 1, 1)
    later = lax.broadcasted_iota(jnp.int32, (LR, LR), 1) >= lax.broadcasted_iota(jnp.int32, (LR, LR), 0)
    lower = lower_lanes(LR)
    live = (lax.broadcasted_iota(jnp.int32, (LR, 128), 0) < length).astype(F32)
    features = HEADS * HDIM
    diagonal = lax.broadcasted_iota(jnp.int32, (LR, LR), 1) == lax.broadcasted_iota(jnp.int32, (LR, LR), 0)
    squares = jnp.sum(jnp.where(diagonal, norm_ref[0, 0:1, :], 0.0), axis=1, keepdims=True)
    inner = jnp.sum(jnp.where(diagonal, norm_ref[0, 1:2, :], 0.0), axis=1, keepdims=True)
    factor = lax.rsqrt(squares / features + 1e-05)
    scaled = factor * factor * factor * inner / features
    fade = fade_t[0, 0]
    source = source_t[0, 0]
    grad_meeting = jnp.zeros((LR, LR), F32)
    row_parts = []
    column_parts = []
    faded = []
    for pair in range(x_ref.shape[2] // 128):
        lanes = slice(pair * 128, (pair + 1) * 128)
        raw = raw_ref[0, :, lanes]
        gain = gain_ref[:, lanes]
        out_ref[0, :, lanes] = (raw * factor * gain).astype(BF16)
        grad = (factor * (cot_ref[0, :, lanes].astype(F32) * gain) - raw * scaled) * live
        grad_pair = split(grad)
        x = x_ref[0, :, lanes]
        zero = jnp.zeros_like(x)
        x_both = jnp.concatenate([jnp.where(lower, x, zero), jnp.where(lower, zero, x)], axis=0)
        grad_mixing = dot(x_both, grad_pair[0], 1, 1) + dot(x_both, grad_pair[1], 1, 1)
        mixing = []
        for i in range(2):
            head = 2 * pair + i
            exponent = decay[0, head : head + 1, :] - source[:, head : head + 1]
            table = jnp.exp(jnp.where(later, exponent, -1e30))
            grad_meeting += grad_mixing[i * LR : (i + 1) * LR] * table
            mixing.append(table * meeting)
        both = dot3(split(jnp.concatenate(mixing, axis=0)), grad_pair, 1, 0)
        grad_x = jnp.where(lower, both[:LR], both[LR:])
        gx_ref[0, :, lanes] = grad_x.astype(BF16)
        row_parts.append(grad * raw)
        column_parts.append(grad_x * x.astype(F32))
        fading = jnp.where(lower, fade[:, 2 * pair : 2 * pair + 1], fade[:, 2 * pair + 1 : 2 * pair + 2])
        faded.append(grad * fading)
    rows_ref[0] = head_sums(jnp.concatenate(row_parts, axis=1))
    columns_ref[0] = head_sums(jnp.concatenate(column_parts, axis=1))
    faded = split(jnp.concatenate(faded, axis=1))
    meeting_pair = split(grad_meeting)
    gb_ref[0] = (dot(meeting_pair[0], c, 1, 0) + dot(meeting_pair[1], c, 1, 0)).astype(BF16)
    grad_c = dot(meeting_pair[0], b, 0, 0) + dot(meeting_pair[1], b, 0, 0)
    gc_ref[0] = (grad_c + dot3(faded, state, 1, 1)).astype(BF16)
    grad_state = dot(c, faded[0], 0, 0) + dot(c, faded[1], 0, 0)
    for number, (upper_out, lower_out) in enumerate(((g1, g1), (g2a, g2b), (g3, g3))):
        share = (offset == number + 1).astype(F32)
        upper = pl.ds(0, STATE // 2)
        lower = pl.ds(lower_out.shape[0] - STATE // 2, STATE // 2)

        @pl.when(reply == 0)
        def _():
            upper_out[upper] = grad_state[: STATE // 2] * share
            lower_out[lower] = grad_state[STATE // 2 :] * share

        @pl.when(reply > 0)
        def _():
            upper_out[upper] += grad_state[: STATE // 2] * share
            lower_out[lower] += grad_state[STATE // 2 :] * share


def ssm_backward(meta, raw, x, cot, gain, b, c, norm, fade_t, source_t, decay, states, group, before):
    replies, length, full = x.shape
    width = full // 2
    heads = width // HDIM
    wide = pl.BlockSpec((1, length, width), lambda r, m: (r, 0, group))
    own = pl.BlockSpec((1, length, width), lambda r, m: (r, 0, 0))
    thin = pl.BlockSpec((1, length, STATE), lambda r, m: (r, 0, group))
    columns = pl.BlockSpec((1, 1, length, heads), lambda r, m: (r, group, 0, 0))
    sums = pl.BlockSpec((1, length, heads), lambda r, m: (r, 0, 0))
    inputs = [raw, x, cot, gain, b, c, norm, fade_t, source_t, decay, *states]
    in_specs = [
        own,
        wide,
        wide,
        pl.BlockSpec((1, width), lambda r, m: (0, group)),
        thin,
        thin,
        pl.BlockSpec((1, 2, length), lambda r, m: (r, 0, 0)),
        columns,
        columns,
        pl.BlockSpec((1, heads, length), lambda r, m: (r, group, 0)),
    ] + state_specs(width)
    aliases = {}
    if before is not None:
        aliases = {1 + len(inputs) + i: i for i in range(4)}
        inputs += before
        in_specs += [pl.BlockSpec(memory_space=pl.ANY)] * 4
    whole = jax.ShapeDtypeStruct((STATE, width), F32)
    half = jax.ShapeDtypeStruct((STATE // 2, width), F32)
    outs = pl.pallas_call(
        ssm_backward_body,
        grid_spec=pltpu.PrefetchScalarGridSpec(
            num_scalar_prefetch=1,
            grid=(replies,),
            in_specs=in_specs,
            out_specs=[wide, wide, thin, thin, sums, sums] + state_specs(width),
        ),
        out_shape=[
            jax.ShapeDtypeStruct(x.shape, BF16),
            jax.ShapeDtypeStruct(x.shape, BF16),
            jax.ShapeDtypeStruct(b.shape, BF16),
            jax.ShapeDtypeStruct(b.shape, BF16),
            jax.ShapeDtypeStruct((replies, length, heads), F32),
            jax.ShapeDtypeStruct((replies, length, heads), F32),
        ]
        + [whole, half, half, whole],
        input_output_aliases=aliases,
        compiler_params=params(60),
        name="ssm_backward",
    )(meta, *inputs)
    return outs[:4], outs[4], outs[5], (outs[6], outs[7:9], outs[9])


def prompt_grad_body(x_ref, b_ref, w_ref, grad_ref, *rest):
    gx_ref, gmap_ref, sums_ref = rest[-3:]
    grad = split(grad_ref[...])
    x = x_ref[...].astype(F32)
    weight = spread(w_ref[0], lower_lanes(x.shape[0]))
    b = b_ref[...]
    pulled = dot(b, grad[0], 1, 0) + dot(b, grad[1], 1, 0)
    gx_ref[...] = (weight * pulled).astype(BF16)
    gmap_ref[...] = dot3(split(weight * x), grad, 1, 1).astype(BF16)
    sums_ref[...] = head_sums(x * pulled)


def prompt_grad(x, b, w, grad, group, before):
    width = x.shape[1] // 2
    heads = width // HDIM
    rows = 256
    inputs = [x, b, w, grad]
    in_specs = [
        pl.BlockSpec((rows, width), lambda i: (i, group)),
        pl.BlockSpec((rows, STATE), lambda i: (i, group)),
        pl.BlockSpec((1, rows, heads), lambda i: (group, i, 0)),
        pl.BlockSpec((STATE, width), lambda i: (0, 0)),
    ]
    aliases = {}
    if before is not None:
        aliases = {len(inputs) + i: i for i in range(2)}
        inputs += before
        in_specs += [pl.BlockSpec(memory_space=pl.ANY)] * 2
    outs = pl.pallas_call(
        prompt_grad_body,
        grid=(LP // rows,),
        in_specs=in_specs,
        out_specs=[
            pl.BlockSpec((rows, width), lambda i: (i, group)),
            pl.BlockSpec((rows, STATE), lambda i: (i, group)),
            pl.BlockSpec((rows, heads), lambda i: (i, 0)),
        ],
        out_shape=[
            jax.ShapeDtypeStruct(x.shape, BF16),
            jax.ShapeDtypeStruct(b.shape, BF16),
            jax.ShapeDtypeStruct((LP, heads), F32),
        ],
        input_output_aliases=aliases,
        compiler_params=params(40),
        name="prompt_grad",
    )(*inputs)
    return outs[:2], outs[2]


def tables(count):
    last = ROW - 1
    across = [(i, (i + ROW) % count) for i in range(count) if i % ROW == last]
    ahead = [(i, i + 1 if i % ROW != last else i - last) for i in range(count)]
    behind = [(i, (i + last) % count if i % ROW != last else i - 1) for i in range(count)]
    forward = [(i, (i + 1) % count) for i in range(count)]
    return across, ahead, behind, forward


def turned(pairs):
    return [(b, a) for a, b in pairs]


def move(part, pairs):
    return lax.ppermute(part, "seq", pairs)


def merge(part, moved, is_last):
    return jnp.where(is_last, 0.0, part) + moved


def together(*values):
    return lax.optimization_barrier(values)


def columns_of(rows):
    heads, tokens = rows.shape[-2:]
    cut = rows.reshape(rows.shape[:-2] + (2, heads // 2, tokens))
    return jnp.swapaxes(cut, -1, -2)


def shards(
    prompt_x,
    prompt_b,
    prompt_dt,
    prompt_keys,
    prompt_values,
    prompt_len,
    reply_x,
    reply_b,
    reply_c,
    reply_dt,
    reply_queries,
    reply_keys,
    reply_values,
    reply_len,
    reply_owner,
    decay_log,
    step_bias,
    norm_gain,
    ssm_cotangent,
    attn_cotangent,
):
    seq_count = lax.axis_size("seq")
    position = lax.axis_index("seq")
    pairs = tables(seq_count)
    is_last = position % ROW == ROW - 1

    across, ahead, behind, forward = pairs
    backward = turned(forward)
    keys = prompt_keys[0].astype(F32)
    mark = jnp.full((MARK, keys.shape[1]), prompt_len[0].astype(F32))
    own = jnp.concatenate([mark, keys, prompt_values[0].astype(F32)], axis=0)
    own_moved = move(own, across)

    rate = -jnp.exp(decay_log)
    tokens = jnp.arange(LP)
    prompt_raw = prompt_dt[0].astype(F32) + step_bias[:, None]
    prompt_plus = jax.nn.softplus(prompt_raw)
    prompt_valid = (tokens < prompt_len[0]).astype(F32)[None, :]
    prompt_steps = prompt_plus * prompt_valid
    after = (tokens[:, None] > tokens[None, :]).astype(F32)
    remaining = jnp.einsum("hu,us->hs", prompt_steps, after, precision=HIGHEST)
    weight = prompt_steps * jnp.exp(rate[:, None] * remaining)
    weight_t = columns_of(weight)
    state = [prompt_state(prompt_x[0], prompt_b[0], weight_t, group) for group in range(2)]

    times = jnp.arange(LR)
    reply_raw = reply_dt.astype(F32) + step_bias[None, :, None]
    reply_plus = jax.nn.softplus(reply_raw)
    reply_valid = (times[None, :] < reply_len[:, None])[:, None, :]
    reply_steps = jnp.where(reply_valid, reply_plus, 0.0)
    until = (times[:, None] <= times[None, :]).astype(F32)
    running = jnp.einsum("rhu,ut->rht", reply_steps, until, precision=HIGHEST)
    decay = rate[None, :, None] * running
    source = decay - jnp.where(reply_valid, jnp.log(reply_plus), -1e30)
    decay_t = columns_of(decay)
    fade_t = jnp.exp(decay_t)
    source_t = columns_of(source)

    offsets = (position - reply_owner) % seq_count
    meta = jnp.concatenate([offsets, reply_len]).astype(jnp.int32)

    gain = norm_gain[None, :]
    key_cut = MARK + LP
    cut = STATE // 2

    def spread_out(one, three, at):
        return move(one[:at], forward), move(three[at:], backward)

    def gather_in(parts):
        return move(parts[1][0], backward), move(parts[1][1], forward)

    def homeward(parts, came):
        at = came[0].shape[0]
        one = jnp.concatenate([parts[0][:at] + came[0], parts[0][at:]], axis=0)
        three = jnp.concatenate([parts[2][:at], parts[2][at:] + came[1]], axis=0)
        return move(one, turned(ahead)), move(three, turned(behind))

    own = merge(own, own_moved, is_last)
    own, first = together(own, state[0])
    own_one, own_three = move(own, ahead), move(own, behind)
    first_moved = move(first, across)

    first = merge(first, first_moved, is_last)
    own_one, own_three, first, second = together(own_one, own_three, first, state[1])
    own_two = spread_out(own_one, own_three, key_cut)
    first_one, first_three = move(first, ahead), move(first, behind)
    second_moved = move(second, across)

    second = merge(second, second_moved, is_last)
    own_two, first_one, first_three, second, queries = together(
        own_two, first_one, first_three, second, reply_queries
    )
    first_two = spread_out(first_one, first_three, cut)
    second_one, second_three = move(second, ahead), move(second, behind)
    (attn_output, grad_queries, grad_keys, grad_values), own_parts = attention(
        meta, queries, attn_cotangent, reply_keys, reply_values, own_one, own_two, own_three
    )

    first_two, second_one, second_three, own_parts, x = together(
        first_two, second_one, second_three, own_parts, reply_x
    )
    second_two = spread_out(second_one, second_three, cut)
    states = [(first_one, *first_two, first_three), (second_one, *second_two, second_three)]

    def forward_part(group, x, before):
        return ssm_forward(
            meta, x, ssm_cotangent, gain, reply_b, reply_c, decay_t, fade_t, source, states[group], before, group
        )

    def backward_part(group, raw, before):
        return ssm_backward(
            meta, raw, reply_x, ssm_cotangent, gain, reply_b, reply_c, sums, fade_t, source_t, decay,
            states[group], group, before,
        )

    raw_first, sums = forward_part(0, x, jnp.zeros((reply_x.shape[0], 2, LR), F32))

    raw_first, own_parts = together(raw_first, own_parts)
    own_came = gather_in(own_parts)
    states[1], x = together(states[1], x)
    raw_second, sums = forward_part(1, x, sums)
    sums = lax.psum(sums, "head")
    own_came, own_parts, _ = together(own_came, own_parts, sums)
    own_home = homeward(own_parts, own_came)
    wide, rows_first, columns_first, first_parts = backward_part(0, raw_first, None)

    first_parts, raw_second = together(first_parts, raw_second)
    first_came = gather_in(first_parts)
    wide, rows_second, columns_second, second_parts = backward_part(1, raw_second, wide)
    ssm_output, grad_x, grad_b, grad_c = wide
    rows = [rows_first, rows_second]
    columns = [columns_first, columns_second]

    first_came, second_parts, own_home = together(first_came, second_parts, own_home)
    first_home = homeward(first_parts, first_came)
    second_came = gather_in(second_parts)
    own_total = own_home[0] + own_home[1]
    own_last = move(own_total, turned(across))

    first_home, second_came, own_last = together(first_home, second_came, own_last)
    own_total = merge(own_total, own_last, is_last)
    grad_prompt_keys, grad_prompt_values = own_total[:LP], own_total[LP:]
    second_home = homeward(second_parts, second_came)
    first_total = first_home[0] + first_home[1]
    first_last = move(first_total, turned(across))

    second_total = second_home[0] + second_home[1]
    second_last = move(second_total, turned(across))
    grads = [merge(first_total, first_last, is_last), merge(second_total, second_last, is_last)]

    rows = jnp.concatenate(rows, axis=-1)
    columns = jnp.concatenate(columns, axis=-1)
    grad_running = rate * (rows - columns)
    grad_steps = jnp.einsum("rth,ut->rhu", grad_running, until, precision=HIGHEST)
    grad_steps += jnp.swapaxes(columns, 1, 2) / reply_plus
    grad_reply_dt = jnp.where(reply_valid, grad_steps * jax.nn.sigmoid(reply_raw), 0.0).astype(BF16)

    wide = None
    shares = []
    for group in range(2):
        wide, share = prompt_grad(prompt_x[0], prompt_b[0], weight_t, grads[group], group, wide)
        shares.append(share)
    grad_px, grad_pb = wide
    share = jnp.concatenate(shares, axis=-1).T * weight
    earlier = jnp.einsum("hs,su->hu", share, after.T, precision=HIGHEST)
    grad_prompt_steps = share / prompt_plus + rate[:, None] * earlier
    grad_prompt_dt = (grad_prompt_steps * prompt_valid * jax.nn.sigmoid(prompt_raw)).astype(BF16)

    return (
        ssm_output,
        attn_output,
        grad_x,
        grad_b,
        grad_c,
        grad_reply_dt,
        grad_queries,
        grad_keys,
        grad_values,
        grad_px[None],
        grad_pb[None],
        grad_prompt_dt[None],
        grad_prompt_keys.astype(BF16)[None],
        grad_prompt_values.astype(BF16)[None],
    )


def solution(mesh):
    placed = (
        P("seq", None, "head"),
        P("seq", None, "head"),
        P("seq", "head", None),
        P("seq", None, "head"),
        P("seq", None, "head"),
        P("seq"),
        P("seq", None, "head"),
        P("seq", None, "head"),
        P("seq", None, "head"),
        P("seq", "head", None),
        P("seq", None, "head"),
        P("seq", None, "head"),
        P("seq", None, "head"),
        P("seq"),
        P("seq"),
        P("head"),
        P("head"),
        P("head"),
        P("seq", None, "head"),
        P("seq", None, "head"),
    )
    return jax.shard_map(
        shards,
        mesh=mesh,
        in_specs=placed,
        out_specs=(
            P("seq", None, "head"),
            P("seq", None, "head"),
            P("seq", None, "head"),
            P("seq", None, "head"),
            P("seq", None, "head"),
            P("seq", "head", None),
            P("seq", None, "head"),
            P("seq", None, "head"),
            P("seq", None, "head"),
            P("seq", None, "head"),
            P("seq", None, "head"),
            P("seq", "head", None),
            P("seq", None, "head"),
            P("seq", None, "head"),
        ),
        check_vma=False,
    )
```

```python
import jax
import jax.numpy as jnp
from jax import lax
from jax.experimental import pallas as pl
from jax.experimental.pallas import tpu as pltpu
from jax.sharding import PartitionSpec as P

HEADS = 128
HDIM = 64
STATE = 128
AHDIM = 128
OFFSETS = 3
LP = 512
LR = 128
MARK = 8
ROW = 4

HIGHEST = lax.Precision.HIGHEST
F32 = jnp.float32
BF16 = jnp.bfloat16


def split(a):
    hi = a.astype(BF16)
    return hi, (a - hi.astype(F32)).astype(BF16)


def dot(a, b, ca, cb):
    return lax.dot_general(a, b, (((ca,), (cb,)), ((), ())), preferred_element_type=F32)


def dot2(a, b, ca, cb):
    hi, lo = split(a)
    return dot(hi, b, ca, cb) + dot(lo, b, ca, cb)


def dot3(a, b, ca, cb):
    return dot(a[0], b[0], ca, cb) + (dot(a[1], b[0], ca, cb) + dot(a[0], b[1], ca, cb))


def spread(columns, lower):
    parts = []
    for pair in range(columns.shape[1] // 2):
        left = columns[:, 2 * pair : 2 * pair + 1]
        right = columns[:, 2 * pair + 1 : 2 * pair + 2]
        parts.append(jnp.where(lower, left, right))
    return jnp.concatenate(parts, axis=1)


def lower_lanes(rows):
    return lax.broadcasted_iota(jnp.int32, (rows, 128), 1) < HDIM


def head_sums(values):
    width = values.shape[1]
    row = lax.broadcasted_iota(jnp.int32, (width, width // HDIM), 0)
    column = lax.broadcasted_iota(jnp.int32, (width, width // HDIM), 1)
    ones = ((row >= column * HDIM) & (row < (column + 1) * HDIM)).astype(F32).astype(BF16)
    return dot2(values, ones, 1, 0)


def params(mebibytes):
    return pltpu.CompilerParams(vmem_limit_bytes=mebibytes * 1024 * 1024)


def prompt_state_body(x_ref, b_ref, w_ref, out_ref):
    step = pl.program_id(0)
    weighted = spread(w_ref[0], lower_lanes(x_ref.shape[0])) * x_ref[...].astype(F32)
    hi, lo = split(weighted)
    result = dot(b_ref[...], hi, 0, 0) + dot(b_ref[...], lo, 0, 0)

    @pl.when(step == 0)
    def _():
        out_ref[...] = result

    @pl.when(step > 0)
    def _():
        out_ref[...] += result


def prompt_state(x, b, w, group):
    width = x.shape[1] // 2
    rows = 256
    return pl.pallas_call(
        prompt_state_body,
        grid=(LP // rows,),
        in_specs=[
            pl.BlockSpec((rows, width), lambda i: (i, group)),
            pl.BlockSpec((rows, STATE), lambda i: (i, group)),
            pl.BlockSpec((1, rows, width // HDIM), lambda i: (group, i, 0)),
        ],
        out_specs=pl.BlockSpec((STATE, width), lambda i: (0, 0)),
        out_shape=jax.ShapeDtypeStruct((STATE, width), F32),
        compiler_params=params(40),
        name="prompt_state",
    )(x, b, w)


def pick(offset, one, two, three):
    return jnp.where(offset == 1, one, jnp.where(offset == 2, two, three))


def attention_body(
    meta, q_ref, cot_ref, k_ref, v_ref, kv1, k2, v2, kv3,
    out_ref, gq_ref, gk_ref, gv_ref, g1, gk2, gv2, g3,
):
    reply = pl.program_id(1)
    offset = meta[reply]
    length = meta[2 + reply]
    given = pick(offset, kv1[: MARK + LP], k2[...], kv3[: MARK + LP])
    prior = jnp.concatenate([given[0:1]] * ((LP + LR) // AHDIM), axis=1).astype(jnp.int32)
    keys = jnp.concatenate([given[MARK:].astype(BF16), k_ref[0]], axis=0)
    given = pick(offset, kv1[MARK + LP :], v2[...], kv3[MARK + LP :])
    values = jnp.concatenate([given.astype(BF16), v_ref[0]], axis=0)
    scale = AHDIM ** (-0.5)
    heads = 2
    rows = heads * LR
    total = LP + LR
    token = lax.broadcasted_iota(jnp.int32, (rows, total), 0) % LR
    key = lax.broadcasted_iota(jnp.int32, (rows, total), 1)
    own = key - LP
    allowed = ((key < LP) & (key < prior)) | ((own >= 0) & (own <= token) & (own < length))
    live = (lax.broadcasted_iota(jnp.int32, (rows, AHDIM), 0) % LR < length).astype(F32)
    grad_keys = jnp.zeros((total, AHDIM), F32)
    grad_values = jnp.zeros((total, AHDIM), F32)
    for part in range(8 // heads):
        lanes = [slice((part * heads + i) * AHDIM, (part * heads + i + 1) * AHDIM) for i in range(heads)]
        query = jnp.concatenate([q_ref[0, :, at] for at in lanes], axis=0)
        grad_out = jnp.concatenate([cot_ref[0, :, at] for at in lanes], axis=0)
        grad_out = (grad_out.astype(F32) * live).astype(BF16)
        scores = jnp.where(allowed, dot(query, keys, 1, 1) * scale, -1e30)
        top = jnp.max(scores, axis=1, keepdims=True)
        weights = jnp.exp(scores - top)
        weights = weights * (1.0 / jnp.sum(weights, axis=1, keepdims=True))
        weights_hi, weights_lo = split(weights)
        out = dot(weights_hi, values, 1, 0) + dot(weights_lo, values, 1, 0)
        inner = jnp.sum(out * grad_out.astype(F32), axis=1, keepdims=True)
        grad_scores = weights * (dot(grad_out, values, 1, 1) - inner) * scale
        grad_hi, grad_lo = split(grad_scores)
        grad_query = dot(grad_hi, keys, 1, 0) + dot(grad_lo, keys, 1, 0)
        grad_keys += dot(grad_hi, query, 0, 0) + dot(grad_lo, query, 0, 0)
        grad_values += dot(weights_hi, grad_out, 0, 0) + dot(weights_lo, grad_out, 0, 0)
        out = out * live
        for i, at in enumerate(lanes):
            out_ref[0, :, at] = out[i * LR : (i + 1) * LR].astype(BF16)
            gq_ref[0, :, at] = grad_query[i * LR : (i + 1) * LR].astype(BF16)
    gk_ref[0] = grad_keys[LP:].astype(BF16)
    gv_ref[0] = grad_values[LP:].astype(BF16)
    for number, (key_out, value_out) in enumerate(((g1, g1), (gk2, gv2), (g3, g3))):
        share = (offset == number + 1).astype(F32)
        key_rows = pl.ds(0, LP)
        value_rows = pl.ds(value_out.shape[0] - LP, LP)

        @pl.when(reply == 0)
        def _():
            key_out[key_rows] = grad_keys[:LP] * share
            value_out[value_rows] = grad_values[:LP] * share

        @pl.when(reply > 0)
        def _():
            key_out[key_rows] += grad_keys[:LP] * share
            value_out[value_rows] += grad_values[:LP] * share


def attention(meta, q, cot, k, v, one, two, three):
    replies, length, width = q.shape
    kv_heads = k.shape[2] // AHDIM
    wide = width // kv_heads
    by_reply = lambda size: pl.BlockSpec((1, length, size), lambda h, r, m: (r, 0, h))
    prior = lambda rows: pl.BlockSpec((rows, AHDIM), lambda h, r, m: (0, h))
    prior_shape = lambda rows: jax.ShapeDtypeStruct((rows, k.shape[2]), F32)
    out_rows = (2 * LP, LP, LP, 2 * LP)
    outs = pl.pallas_call(
        attention_body,
        grid_spec=pltpu.PrefetchScalarGridSpec(
            num_scalar_prefetch=1,
            grid=(kv_heads, replies),
            in_specs=[by_reply(wide), by_reply(wide), by_reply(AHDIM), by_reply(AHDIM)]
            + [prior(MARK + 2 * LP), prior(MARK + LP), prior(LP), prior(MARK + 2 * LP)],
            out_specs=[by_reply(wide), by_reply(wide), by_reply(AHDIM), by_reply(AHDIM)]
            + [prior(rows) for rows in out_rows],
        ),
        out_shape=[
            jax.ShapeDtypeStruct(q.shape, BF16),
            jax.ShapeDtypeStruct(q.shape, BF16),
            jax.ShapeDtypeStruct(k.shape, BF16),
            jax.ShapeDtypeStruct(k.shape, BF16),
        ]
        + [prior_shape(rows) for rows in out_rows],
        compiler_params=params(60),
        name="attention",
    )(meta, q, cot, k, v, one, *two, three)
    return outs[:4], (outs[4], outs[5:7], outs[7])


def carried_state(offset, one, two_upper, two_lower, three):
    two = jnp.concatenate([two_upper[...], two_lower[...]], axis=0)
    return split(pick(offset, one[...], two, three[...]))


def ssm_forward_body(
    meta, x_ref, cot_ref, gain_ref, b_ref, c_ref, decay_t, fade_t, source,
    s1, s2a, s2b, s3, before_ref, raw_ref, sums_ref,
):
    reply = pl.program_id(0)
    length = meta[2 + reply]
    state = carried_state(meta[reply], s1, s2a, s2b, s3)
    c = c_ref[0]
    meeting = dot(c, b_ref[0], 1, 1)
    causal = lax.broadcasted_iota(jnp.int32, (LR, LR), 0) >= lax.broadcasted_iota(jnp.int32, (LR, LR), 1)
    lower = lower_lanes(LR)
    live = (lax.broadcasted_iota(jnp.int32, (LR, 128), 0) < length).astype(F32)
    carried = dot(c, state[0], 1, 0) + dot(c, state[1], 1, 0)
    decay = decay_t[0, 0]
    fade = fade_t[0, 0]
    squares = jnp.zeros((LR, 128), F32)
    inner = jnp.zeros((LR, 128), F32)
    for pair in range(x_ref.shape[2] // 128):
        lanes = slice(pair * 128, (pair + 1) * 128)
        mixing = []
        for head in (2 * pair, 2 * pair + 1):
            exponent = decay[:, head : head + 1] - source[0, head : head + 1, :]
            mixing.append(jnp.exp(jnp.where(causal, exponent, -1e30)) * meeting)
        both = dot2(jnp.concatenate(mixing, axis=0), x_ref[0, :, lanes], 1, 0)
        local = jnp.where(lower, both[:LR], both[LR:])
        fading = jnp.where(lower, fade[:, 2 * pair : 2 * pair + 1], fade[:, 2 * pair + 1 : 2 * pair + 2])
        raw = (local + carried[:, lanes] * fading) * live
        raw_ref[0, :, lanes] = raw
        squares += raw * raw
        inner += cot_ref[0, :, lanes].astype(F32) * gain_ref[:, lanes] * raw
    ones = jnp.ones((8, 128), BF16)
    for row, partial in enumerate((squares, inner)):
        hi, lo = split(partial)
        sums_ref[0, row : row + 1, :] = (dot(ones, hi, 1, 1) + dot(ones, lo, 1, 1))[0:1] + before_ref[0, row : row + 1, :]


def state_specs(width):
    return [pl.BlockSpec((rows, width), lambda r, m: (0, 0)) for rows in (STATE, STATE // 2, STATE // 2, STATE)]


def ssm_forward(meta, x, cot, gain, b, c, decay_t, fade_t, source, states, before, group):
    replies, length, width = x.shape
    width //= 2
    heads = width // HDIM
    wide = pl.BlockSpec((1, length, width), lambda r, m: (r, 0, group))
    thin = pl.BlockSpec((1, length, STATE), lambda r, m: (r, 0, group))
    columns = pl.BlockSpec((1, 1, length, heads), lambda r, m: (r, group, 0, 0))
    sums = pl.BlockSpec((1, 2, length), lambda r, m: (r, 0, 0))
    return pl.pallas_call(
        ssm_forward_body,
        grid_spec=pltpu.PrefetchScalarGridSpec(
            num_scalar_prefetch=1,
            grid=(replies,),
            in_specs=[
                wide,
                wide,
                pl.BlockSpec((1, width), lambda r, m: (0, group)),
                thin,
                thin,
                columns,
                columns,
                pl.BlockSpec((1, heads, length), lambda r, m: (r, group, 0)),
            ]
            + state_specs(width)
            + [sums],
            out_specs=[pl.BlockSpec((1, length, width), lambda r, m: (r, 0, 0)), sums],
        ),
        out_shape=[
            jax.ShapeDtypeStruct((replies, length, width), F32),
            jax.ShapeDtypeStruct((replies, 2, length), F32),
        ],
        compiler_params=params(60),
        name="ssm_forward",
    )(meta, x, cot, gain, b, c, decay_t, fade_t, source, *states, before)


def ssm_backward_body(
    meta, raw_ref, x_ref, cot_ref, gain_ref, b_ref, c_ref, norm_ref, fade_t, source_t, decay,
    s1, s2a, s2b, s3, *rest,
):
    out_ref, gx_ref, gb_ref, gc_ref, rows_ref, columns_ref, g1, g2a, g2b, g3 = rest[-10:]
    reply = pl.program_id(0)
    offset = meta[reply]
    length = meta[2 + reply]
    state = carried_state(offset, s1, s2a, s2b, s3)
    b = b_ref[0]
    c = c_ref[0]
    meeting = dot(b, c, 1, 1)
    later = lax.broadcasted_iota(jnp.int32, (LR, LR), 1) >= lax.broadcasted_iota(jnp.int32, (LR, LR), 0)
    lower = lower_lanes(LR)
    live = (lax.broadcasted_iota(jnp.int32, (LR, 128), 0) < length).astype(F32)
    features = HEADS * HDIM
    diagonal = lax.broadcasted_iota(jnp.int32, (LR, LR), 1) == lax.broadcasted_iota(jnp.int32, (LR, LR), 0)
    squares = jnp.sum(jnp.where(diagonal, norm_ref[0, 0:1, :], 0.0), axis=1, keepdims=True)
    inner = jnp.sum(jnp.where(diagonal, norm_ref[0, 1:2, :], 0.0), axis=1, keepdims=True)
    factor = lax.rsqrt(squares / features + 1e-05)
    scaled = factor * factor * factor * inner / features
    fade = fade_t[0, 0]
    source = source_t[0, 0]
    grad_meeting = jnp.zeros((LR, LR), F32)
    row_parts = []
    column_parts = []
    faded = []
    for pair in range(x_ref.shape[2] // 128):
        lanes = slice(pair * 128, (pair + 1) * 128)
        raw = raw_ref[0, :, lanes]
        gain = gain_ref[:, lanes]
        out_ref[0, :, lanes] = (raw * factor * gain).astype(BF16)
        grad = (factor * (cot_ref[0, :, lanes].astype(F32) * gain) - raw * scaled) * live
        grad_pair = split(grad)
        x = x_ref[0, :, lanes]
        zero = jnp.zeros_like(x)
        x_both = jnp.concatenate([jnp.where(lower, x, zero), jnp.where(lower, zero, x)], axis=0)
        grad_mixing = dot(x_both, grad_pair[0], 1, 1) + dot(x_both, grad_pair[1], 1, 1)
        mixing = []
        for i in range(2):
            head = 2 * pair + i
            exponent = decay[0, head : head + 1, :] - source[:, head : head + 1]
            table = jnp.exp(jnp.where(later, exponent, -1e30))
            grad_meeting += grad_mixing[i * LR : (i + 1) * LR] * table
            mixing.append(table * meeting)
        both = dot3(split(jnp.concatenate(mixing, axis=0)), grad_pair, 1, 0)
        grad_x = jnp.where(lower, both[:LR], both[LR:])
        gx_ref[0, :, lanes] = grad_x.astype(BF16)
        row_parts.append(grad * raw)
        column_parts.append(grad_x * x.astype(F32))
        fading = jnp.where(lower, fade[:, 2 * pair : 2 * pair + 1], fade[:, 2 * pair + 1 : 2 * pair + 2])
        faded.append(grad * fading)
    rows_ref[0] = head_sums(jnp.concatenate(row_parts, axis=1))
    columns_ref[0] = head_sums(jnp.concatenate(column_parts, axis=1))
    faded = split(jnp.concatenate(faded, axis=1))
    meeting_pair = split(grad_meeting)
    gb_ref[0] = (dot(meeting_pair[0], c, 1, 0) + dot(meeting_pair[1], c, 1, 0)).astype(BF16)
    grad_c = dot(meeting_pair[0], b, 0, 0) + dot(meeting_pair[1], b, 0, 0)
    gc_ref[0] = (grad_c + dot3(faded, state, 1, 1)).astype(BF16)
    grad_state = dot(c, faded[0], 0, 0) + dot(c, faded[1], 0, 0)
    for number, (upper_out, lower_out) in enumerate(((g1, g1), (g2a, g2b), (g3, g3))):
        share = (offset == number + 1).astype(F32)
        upper = pl.ds(0, STATE // 2)
        lower = pl.ds(lower_out.shape[0] - STATE // 2, STATE // 2)

        @pl.when(reply == 0)
        def _():
            upper_out[upper] = grad_state[: STATE // 2] * share
            lower_out[lower] = grad_state[STATE // 2 :] * share

        @pl.when(reply > 0)
        def _():
            upper_out[upper] += grad_state[: STATE // 2] * share
            lower_out[lower] += grad_state[STATE // 2 :] * share


def ssm_backward(meta, raw, x, cot, gain, b, c, norm, fade_t, source_t, decay, states, group, before):
    replies, length, full = x.shape
    width = full // 2
    heads = width // HDIM
    wide = pl.BlockSpec((1, length, width), lambda r, m: (r, 0, group))
    own = pl.BlockSpec((1, length, width), lambda r, m: (r, 0, 0))
    thin = pl.BlockSpec((1, length, STATE), lambda r, m: (r, 0, group))
    columns = pl.BlockSpec((1, 1, length, heads), lambda r, m: (r, group, 0, 0))
    sums = pl.BlockSpec((1, length, heads), lambda r, m: (r, 0, 0))
    inputs = [raw, x, cot, gain, b, c, norm, fade_t, source_t, decay, *states]
    in_specs = [
        own,
        wide,
        wide,
        pl.BlockSpec((1, width), lambda r, m: (0, group)),
        thin,
        thin,
        pl.BlockSpec((1, 2, length), lambda r, m: (r, 0, 0)),
        columns,
        columns,
        pl.BlockSpec((1, heads, length), lambda r, m: (r, group, 0)),
    ] + state_specs(width)
    aliases = {}
    if before is not None:
        aliases = {1 + len(inputs) + i: i for i in range(4)}
        inputs += before
        in_specs += [pl.BlockSpec(memory_space=pl.ANY)] * 4
    whole = jax.ShapeDtypeStruct((STATE, width), F32)
    half = jax.ShapeDtypeStruct((STATE // 2, width), F32)
    outs = pl.pallas_call(
        ssm_backward_body,
        grid_spec=pltpu.PrefetchScalarGridSpec(
            num_scalar_prefetch=1,
            grid=(replies,),
            in_specs=in_specs,
            out_specs=[wide, wide, thin, thin, sums, sums] + state_specs(width),
        ),
        out_shape=[
            jax.ShapeDtypeStruct(x.shape, BF16),
            jax.ShapeDtypeStruct(x.shape, BF16),
            jax.ShapeDtypeStruct(b.shape, BF16),
            jax.ShapeDtypeStruct(b.shape, BF16),
            jax.ShapeDtypeStruct((replies, length, heads), F32),
            jax.ShapeDtypeStruct((replies, length, heads), F32),
        ]
        + [whole, half, half, whole],
        input_output_aliases=aliases,
        compiler_params=params(60),
        name="ssm_backward",
    )(meta, *inputs)
    return outs[:4], outs[4], outs[5], (outs[6], outs[7:9], outs[9])


def prompt_grad_body(x_ref, b_ref, w_ref, grad_ref, *rest):
    gx_ref, gmap_ref, sums_ref = rest[-3:]
    grad = split(grad_ref[...])
    x = x_ref[...].astype(F32)
    weight = spread(w_ref[0], lower_lanes(x.shape[0]))
    b = b_ref[...]
    pulled = dot(b, grad[0], 1, 0) + dot(b, grad[1], 1, 0)
    gx_ref[...] = (weight * pulled).astype(BF16)
    gmap_ref[...] = dot3(split(weight * x), grad, 1, 1).astype(BF16)
    sums_ref[...] = head_sums(x * pulled)


def prompt_grad(x, b, w, grad, group, before):
    width = x.shape[1] // 2
    heads = width // HDIM
    rows = 512
    inputs = [x, b, w, grad]
    in_specs = [
        pl.BlockSpec((rows, width), lambda i: (i, group)),
        pl.BlockSpec((rows, STATE), lambda i: (i, group)),
        pl.BlockSpec((1, rows, heads), lambda i: (group, i, 0)),
        pl.BlockSpec((STATE, width), lambda i: (0, 0)),
    ]
    aliases = {}
    if before is not None:
        aliases = {len(inputs) + i: i for i in range(2)}
        inputs += before
        in_specs += [pl.BlockSpec(memory_space=pl.ANY)] * 2
    outs = pl.pallas_call(
        prompt_grad_body,
        grid=(LP // rows,),
        in_specs=in_specs,
        out_specs=[
            pl.BlockSpec((rows, width), lambda i: (i, group)),
            pl.BlockSpec((rows, STATE), lambda i: (i, group)),
            pl.BlockSpec((rows, heads), lambda i: (i, 0)),
        ],
        out_shape=[
            jax.ShapeDtypeStruct(x.shape, BF16),
            jax.ShapeDtypeStruct(b.shape, BF16),
            jax.ShapeDtypeStruct((LP, heads), F32),
        ],
        input_output_aliases=aliases,
        compiler_params=params(40),
        name="prompt_grad",
    )(*inputs)
    return outs[:2], outs[2]


def tables(count):
    last = ROW - 1
    across = [(i, (i + ROW) % count) for i in range(count) if i % ROW == last]
    ahead = [(i, i + 1 if i % ROW != last else i - last) for i in range(count)]
    behind = [(i, (i + last) % count if i % ROW != last else i - 1) for i in range(count)]
    forward = [(i, (i + 1) % count) for i in range(count)]
    return across, ahead, behind, forward


def turned(pairs):
    return [(b, a) for a, b in pairs]


def move(part, pairs):
    return lax.ppermute(part, "seq", pairs)


def merge(part, moved, is_last):
    return jnp.where(is_last, 0.0, part) + moved


def together(*values):
    return lax.optimization_barrier(values)


def columns_of(rows):
    heads, tokens = rows.shape[-2:]
    cut = rows.reshape(rows.shape[:-2] + (2, heads // 2, tokens))
    return jnp.swapaxes(cut, -1, -2)


def shards(
    prompt_x,
    prompt_b,
    prompt_dt,
    prompt_keys,
    prompt_values,
    prompt_len,
    reply_x,
    reply_b,
    reply_c,
    reply_dt,
    reply_queries,
    reply_keys,
    reply_values,
    reply_len,
    reply_owner,
    decay_log,
    step_bias,
    norm_gain,
    ssm_cotangent,
    attn_cotangent,
):
    seq_count = lax.axis_size("seq")
    position = lax.axis_index("seq")
    pairs = tables(seq_count)
    is_last = position % ROW == ROW - 1

    across, ahead, behind, forward = pairs
    backward = turned(forward)
    keys = prompt_keys[0].astype(F32)
    mark = jnp.full((MARK, keys.shape[1]), prompt_len[0].astype(F32))
    own = jnp.concatenate([mark, keys, prompt_values[0].astype(F32)], axis=0)
    own_moved = move(own, across)

    rate = -jnp.exp(decay_log)
    tokens = jnp.arange(LP)
    prompt_raw = prompt_dt[0].astype(F32) + step_bias[:, None]
    prompt_plus = jax.nn.softplus(prompt_raw)
    prompt_valid = (tokens < prompt_len[0]).astype(F32)[None, :]
    prompt_steps = prompt_plus * prompt_valid
    after = (tokens[:, None] > tokens[None, :]).astype(F32)
    remaining = jnp.einsum("hu,us->hs", prompt_steps, after, precision=HIGHEST)
    weight = prompt_steps * jnp.exp(rate[:, None] * remaining)
    weight_t = columns_of(weight)
    state = [prompt_state(prompt_x[0], prompt_b[0], weight_t, group) for group in range(2)]

    times = jnp.arange(LR)
    reply_raw = reply_dt.astype(F32) + step_bias[None, :, None]
    reply_plus = jax.nn.softplus(reply_raw)
    reply_valid = (times[None, :] < reply_len[:, None])[:, None, :]
    reply_steps = jnp.where(reply_valid, reply_plus, 0.0)
    until = (times[:, None] <= times[None, :]).astype(F32)
    running = jnp.einsum("rhu,ut->rht", reply_steps, until, precision=HIGHEST)
    decay = rate[None, :, None] * running
    source = decay - jnp.where(reply_valid, jnp.log(reply_plus), -1e30)
    decay_t = columns_of(decay)
    fade_t = jnp.exp(decay_t)
    source_t = columns_of(source)

    offsets = (position - reply_owner) % seq_count
    meta = jnp.concatenate([offsets, reply_len]).astype(jnp.int32)

    gain = norm_gain[None, :]
    key_cut = MARK + LP
    cut = STATE // 2

    def spread_out(one, three, at):
        return move(one[:at], forward), move(three[at:], backward)

    def gather_in(parts):
        return move(parts[1][0], backward), move(parts[1][1], forward)

    def homeward(parts, came):
        at = came[0].shape[0]
        one = jnp.concatenate([parts[0][:at] + came[0], parts[0][at:]], axis=0)
        three = jnp.concatenate([parts[2][:at], parts[2][at:] + came[1]], axis=0)
        return move(one, turned(ahead)), move(three, turned(behind))

    own = merge(own, own_moved, is_last)
    own, first, second = together(own, state[0], state[1])
    own_one, own_three = move(own, ahead), move(own, behind)
    first_moved = move(first, across)
    second_moved = move(second, across)

    first = merge(first, first_moved, is_last)
    own_one, own_three, first = together(own_one, own_three, first)
    own_two = spread_out(own_one, own_three, key_cut)
    first_one, first_three = move(first, ahead), move(first, behind)

    second = merge(second, second_moved, is_last)
    own_two, first_one, first_three, second, queries = together(
        own_two, first_one, first_three, second, reply_queries
    )
    first_two = spread_out(first_one, first_three, cut)
    second_one, second_three = move(second, ahead), move(second, behind)
    (attn_output, grad_queries, grad_keys, grad_values), own_parts = attention(
        meta, queries, attn_cotangent, reply_keys, reply_values, own_one, own_two, own_three
    )

    first_two, second_one, second_three, own_parts, x = together(
        first_two, second_one, second_three, own_parts, reply_x
    )
    second_two = spread_out(second_one, second_three, cut)
    states = [(first_one, *first_two, first_three), (second_one, *second_two, second_three)]

    def forward_part(group, x, before):
        return ssm_forward(
            meta, x, ssm_cotangent, gain, reply_b, reply_c, decay_t, fade_t, source, states[group], before, group
        )

    def backward_part(group, raw, before):
        return ssm_backward(
            meta, raw, reply_x, ssm_cotangent, gain, reply_b, reply_c, sums, fade_t, source_t, decay,
            states[group], group, before,
        )

    raw_first, sums = forward_part(0, x, jnp.zeros((reply_x.shape[0], 2, LR), F32))

    raw_first, own_parts = together(raw_first, own_parts)
    own_came = gather_in(own_parts)
    states[1], x = together(states[1], x)
    raw_second, sums = forward_part(1, x, sums)
    sums = lax.psum(sums, "head")
    own_came, own_parts, _ = together(own_came, own_parts, sums)
    own_home = homeward(own_parts, own_came)
    wide, rows_first, columns_first, first_parts = backward_part(0, raw_first, None)

    first_parts, raw_second = together(first_parts, raw_second)
    first_came = gather_in(first_parts)
    wide, rows_second, columns_second, second_parts = backward_part(1, raw_second, wide)
    ssm_output, grad_x, grad_b, grad_c = wide
    rows = [rows_first, rows_second]
    columns = [columns_first, columns_second]

    first_came, second_parts, own_home = together(first_came, second_parts, own_home)
    first_home = homeward(first_parts, first_came)
    second_came = gather_in(second_parts)
    own_total = own_home[0] + own_home[1]
    own_last = move(own_total, turned(across))

    first_home, second_came, own_last = together(first_home, second_came, own_last)
    own_total = merge(own_total, own_last, is_last)
    grad_prompt_keys, grad_prompt_values = own_total[:LP], own_total[LP:]
    second_home = homeward(second_parts, second_came)
    first_total = first_home[0] + first_home[1]
    first_last = move(first_total, turned(across))

    second_total = second_home[0] + second_home[1]
    second_last = move(second_total, turned(across))
    grads = [merge(first_total, first_last, is_last), merge(second_total, second_last, is_last)]

    rows = jnp.concatenate(rows, axis=-1)
    columns = jnp.concatenate(columns, axis=-1)
    grad_running = rate * (rows - columns)
    grad_steps = jnp.einsum("rth,ut->rhu", grad_running, until, precision=HIGHEST)
    grad_steps += jnp.swapaxes(columns, 1, 2) / reply_plus
    grad_reply_dt = jnp.where(reply_valid, grad_steps * jax.nn.sigmoid(reply_raw), 0.0).astype(BF16)

    wide = None
    shares = []
    for group in range(2):
        wide, share = prompt_grad(prompt_x[0], prompt_b[0], weight_t, grads[group], group, wide)
        shares.append(share)
    grad_px, grad_pb = wide
    share = jnp.concatenate(shares, axis=-1).T * weight
    earlier = jnp.einsum("hs,su->hu", share, after.T, precision=HIGHEST)
    grad_prompt_steps = share / prompt_plus + rate[:, None] * earlier
    grad_prompt_dt = (grad_prompt_steps * prompt_valid * jax.nn.sigmoid(prompt_raw)).astype(BF16)

    return (
        ssm_output,
        attn_output,
        grad_x,
        grad_b,
        grad_c,
        grad_reply_dt,
        grad_queries,
        grad_keys,
        grad_values,
        grad_px[None],
        grad_pb[None],
        grad_prompt_dt[None],
        grad_prompt_keys.astype(BF16)[None],
        grad_prompt_values.astype(BF16)[None],
    )


def solution(mesh):
    placed = (
        P("seq", None, "head"),
        P("seq", None, "head"),
        P("seq", "head", None),
        P("seq", None, "head"),
        P("seq", None, "head"),
        P("seq"),
        P("seq", None, "head"),
        P("seq", None, "head"),
        P("seq", None, "head"),
        P("seq", "head", None),
        P("seq", None, "head"),
        P("seq", None, "head"),
        P("seq", None, "head"),
        P("seq"),
        P("seq"),
        P("head"),
        P("head"),
        P("head"),
        P("seq", None, "head"),
        P("seq", None, "head"),
    )
    return jax.shard_map(
        shards,
        mesh=mesh,
        in_specs=placed,
        out_specs=(
            P("seq", None, "head"),
            P("seq", None, "head"),
            P("seq", None, "head"),
            P("seq", None, "head"),
            P("seq", None, "head"),
            P("seq", "head", None),
            P("seq", None, "head"),
            P("seq", None, "head"),
            P("seq", None, "head"),
            P("seq", None, "head"),
            P("seq", None, "head"),
            P("seq", "head", None),
            P("seq", None, "head"),
            P("seq", None, "head"),
        ),
        check_vma=False,
    )
```
